32 devices in a mesh: node: 8 (over y, x, core), shot: 4 (over z).
Axes of the slice: x: 2, y: 2, z: 4, core: 2. Of those that a mesh axis runs over, the one named last changes fastest.
Arguments:
- spectra: bfloat16 [64, 2, 512, 1024], P(None, None, 'shot', 'node'), may hold values from -6 to 6
- source_block: int32 [6], replicated, may hold values from 0 to 31
- taper_window: int32 [6, 512], replicated, may hold values from 0 to 7
Outputs:
- virtual_gathers: bfloat16 [6, 64, 2, 32, 1024], P(None, 'shot', None, None, 'node')
The draws below stay inside these ranges and needn't reach their ends.
All inputs are finite; a program needn't handle non-finite values.
Results may differ from the reference program's by a relative error of at most 0.0047.
Values may be sent and summed in bfloat16 or wider, within the bound.
A program may use at most 128 MiB of HBM per device.

```python
import jax
import jax.numpy as jnp
from jax import lax

F = 64
SB = 32
ROUNDS = 6
WINDOWS = 8
NODES = 1024
SHOTS = 512


def touch_ends(entries, rng, smallest, top_value):
    extent = entries.shape
    place = [jax.random.randint(jax.random.fold_in(rng, axis), (), 0, extent[axis]) for axis in range(len(extent))]
    entries = entries.at[tuple(place)].set(smallest)
    longest = extent.index(max(extent))
    place[longest] = (place[longest] + 1) % extent[longest]
    return entries.at[tuple(place)].set(top_value)


def level_of(stream_key, shape, cuts, least, top_value):
    loudness, own = 1.0, jax.random.fold_in(stream_key, 6)
    for axis_at, parts in cuts:
        draws = jnp.exp(jax.random.uniform(jax.random.fold_in(own, axis_at), (parts,), jnp.float32, least / len(cuts), top_value / len(cuts)))
        loudness = loudness * jnp.repeat(draws, shape[axis_at] // parts).reshape([-1 if axis == axis_at else 1 for axis in range(len(shape))])
    return loudness


def bell_draw(own_key, shape, deviation, bound, shards=(), dtype=jnp.bfloat16):
    factor_of = level_of(own_key, shape, shards, -0.22, 0.18) if shards else 1.0
    array = jax.random.normal(own_key, shape, jnp.float32) * deviation * factor_of
    return jnp.minimum(jnp.maximum(array, -bound), bound).astype(dtype)


def setup_inputs(seed: int = 0) -> dict:
    splits = jax.random.split(jax.random.key(seed), 4)
    spectra = bell_draw(splits[0], (F, 2, SHOTS, NODES), 1.0, 6.0, ((2, 4), (3, 8)))
    source_block = touch_ends(jax.random.randint(splits[1], (ROUNDS,), 0, NODES // SB), jax.random.fold_in(splits[1], 1), 0, (NODES // SB) - 1).astype(jnp.int32)
    taper_window = touch_ends(jax.random.randint(splits[2], (ROUNDS, SHOTS), 0, WINDOWS), jax.random.fold_in(splits[2], 1), 0, WINDOWS - 1).astype(jnp.int32)
    return {"spectra": spectra, "source_block": source_block, "taper_window": taper_window}


def taper_weights(taper_windows):
    return 0.5 - 0.5 * jnp.cos(jnp.pi * (taper_windows.astype(jnp.float32) + 1.0) / (WINDOWS + 1.0))

def correlate_one(pair):
    tapered_spectra, receiver_nodes = pair
    tap = tapered_spectra.astype(jnp.float32)
    rec = receiver_nodes.astype(jnp.float32)
    high = lax.Precision.HIGHEST
    real = jnp.dot(tap[0].T, rec[0], precision=high) + jnp.dot(tap[1].T, rec[1], precision=high)
    imag = jnp.dot(tap[0].T, rec[1], precision=high) - jnp.dot(tap[1].T, rec[0], precision=high)
    return jnp.stack((real, imag), axis=0)

def reference(spectra, source_block, taper_window):
    shot_weights = taper_weights(taper_window)
    scale = 1.0 / jnp.sqrt(jnp.float32(SHOTS))
    gather_results = []
    for turn in range(ROUNDS):
        offset = (source_block[turn] * SB).astype(jnp.int32)
        block = lax.dynamic_slice_in_dim(spectra, offset, SB, 3)
        tapered_spectra = (block.astype(jnp.float32) * shot_weights[turn][:, None]).astype(jnp.bfloat16)
        summed = lax.map(correlate_one, (tapered_spectra, spectra))
        gather_results.append((summed * scale).astype(jnp.bfloat16))
    return jnp.stack(gather_results, axis=0)
```

```python
import functools

import jax
import jax.numpy as jnp
from jax import lax
from jax.experimental import pallas as pl
from jax.experimental.pallas import tpu as pltpu
from jax.sharding import PartitionSpec as P

SB = 32
WINDOWS = 8
MESH = pl.DeviceIdType.MESH
AHEAD = 4


def taper_weights(taper_windows):
    return 0.5 - 0.5 * jnp.cos(jnp.pi * (taper_windows.astype(jnp.float32) + 1.0) / (WINDOWS + 1.0))


def kernel(
    nodes, groups, stages, scale,
    sel_ref, weight_ref, x_ref, out_ref,
    recv, part, full, *rest,
):
    levels = nodes.bit_length() - 1
    land = rest[:levels]
    own_sem, zs, zr, rs, rr, gs, gr = rest[levels:]
    me = lax.axis_index("node")
    group = lax.axis_index("shot")
    f_dev = recv.shape[0]
    fs = f_dev // stages
    rows = sel_ref.shape[0]
    shots = part.shape[-1]
    unit = part.shape[2]
    per = rows // unit
    rounds = rows // SB
    receivers = recv.shape[-1]

    def peer_at(stride):
        bit = (me // stride) % 2
        return bit, me + stride * (1 - 2 * bit)

    def hop(level, j):
        bit, peer = peer_at(2**level)
        if level:
            bit_odd, peer_odd = peer_at(2 ** (levels - level))
            odd = j % 2
            bit = bit + odd * (bit_odd - bit)
            peer = peer + odd * (peer_odd - peer)
        return bit, peer

    def offset(level, j):
        at = 0
        for lower in range(level):
            at = at + hop(lower, j)[0] * (nodes >> (lower + 1))
        return at

    def spectra_copy(j, d):
        to = (group + d) % groups
        return pltpu.make_async_remote_copy(
            src_ref=x_ref.at[pl.ds(to * f_dev + j * fs, fs)],
            dst_ref=recv.at[pl.ds(j * fs, fs), :, group],
            send_sem=zs.at[j, d - 1],
            recv_sem=zr.at[j, d - 1],
            device_id=(me, to),
            device_id_type=MESH,
        )

    def spectra_arrival(j, d):
        source = (group + groups - d) % groups
        place = recv.at[pl.ds(j * fs, fs), :, source]
        return pltpu.make_async_remote_copy(
            src_ref=place,
            dst_ref=place,
            send_sem=zs.at[j, d - 1],
            recv_sem=zr.at[j, d - 1],
            device_id=(me, source),
            device_id_type=MESH,
        )

    def reduce_copy(level, j):
        bit, peer = hop(level, j)
        size = nodes >> (level + 1)
        return pltpu.make_async_remote_copy(
            src_ref=part.at[j, pl.ds(offset(level, j) + (1 - bit) * size, size)],
            dst_ref=land[level].at[j],
            send_sem=rs.at[level, j],
            recv_sem=rr.at[level, j],
            device_id=(peer, group),
            device_id_type=MESH,
        )

    def gather_copy(level, j, arrival=False):
        bit, peer = hop(level, j)
        size = nodes >> (level + 1)
        half = 1 - bit if arrival else bit
        place = full.at[j, pl.ds(offset(level, j) + half * size, size)]
        return pltpu.make_async_remote_copy(
            src_ref=place,
            dst_ref=place,
            send_sem=gs.at[level, j],
            recv_sem=gr.at[level, j],
            device_id=(peer, group),
            device_id_type=MESH,
        )

    own_copy = pltpu.make_async_copy(
        x_ref.at[pl.ds(group * f_dev, f_dev)], recv.at[:, :, group], own_sem
    )
    own_copy.start()

    barrier = pltpu.get_barrier_semaphore()
    for level in range(levels):
        pl.semaphore_signal(barrier, inc=1, device_id=(peer_at(2**level)[1], group), device_id_type=MESH)
    for d in range(1, groups):
        pl.semaphore_signal(barrier, inc=1, device_id=(me, (group + d) % groups), device_id_type=MESH)
    pl.semaphore_wait(barrier, levels + groups - 1)

    def send_spectra(j):
        for d in range(1, groups):
            spectra_copy(j, d).start()

    for j in range(min(AHEAD, stages)):
        send_spectra(j)
    own_copy.wait()

    def select(j):
        for d in range(1, groups):
            spectra_arrival(j, d).wait_recv()

        @pl.when(j + AHEAD < stages)
        def _():
            send_spectra(j + AHEAD)

        for f in range(fs):
            for c in range(2):
                block = recv[j * fs + f, c].reshape(shots, receivers)
                picked = lax.dot_general(
                    sel_ref[...], block, (((1,), (1,)), ((), ())),
                    preferred_element_type=jnp.float32,
                ).reshape(rounds, SB, shots)
                tapered = (picked * weight_ref[...][:, None, :]).astype(jnp.bfloat16)
                part[j, pl.ds((f * 2 + c) * per, per)] = tapered.reshape(per, unit, shots)
        reduce_copy(0, j).start()

    def reduce(level, j):
        reduce_copy(level, j).wait_recv()
        bit, _ = hop(level, j)
        size = nodes >> (level + 1)
        kept = pl.ds(offset(level, j) + bit * size, size)
        total = part[j, kept] + land[level][j]
        if level + 1 < levels:
            part[j, kept] = total
            reduce_copy(level + 1, j).start()
        else:
            full[j, kept] = total
            gather_copy(level, j).start()

    def correlate(j):
        for f in range(fs):
            first = full[j, pl.ds(2 * f * per, per)].reshape(rows, shots)
            second = full[j, pl.ds((2 * f + 1) * per, per)].reshape(rows, shots)
            both = jnp.concatenate(
                [recv[j * fs + f, c].reshape(shots, receivers) for c in range(2)], axis=1
            )
            by_first = jnp.dot(first, both, preferred_element_type=jnp.float32)
            by_second = jnp.dot(second, both, preferred_element_type=jnp.float32)
            real = (by_first[:, :receivers] + by_second[:, receivers:]) * scale
            imag = (by_first[:, receivers:] - by_second[:, :receivers]) * scale
            out_ref[:, j * fs + f, 0] = real.reshape(rounds, SB, receivers).astype(jnp.bfloat16)
            out_ref[:, j * fs + f, 1] = imag.reshape(rounds, SB, receivers).astype(jnp.bfloat16)

    def gather(level, j):
        gather_copy(level, j, arrival=True).wait_recv()
        if level:
            gather_copy(level - 1, j).start()
        else:
            correlate(j)

    steps = [select]
    steps += [functools.partial(reduce, level) for level in range(levels)]
    steps += [functools.partial(gather, level) for level in reversed(range(levels))]

    @pl.loop(0, stages + len(steps) - 1)
    def _(tick):
        for place in reversed(range(len(steps))):
            j = tick - place
            pl.when((j >= 0) & (j < stages))(functools.partial(steps[place], j))

    @pl.loop(0, stages)
    def _(j):
        for d in range(1, groups):
            spectra_copy(j, d).wait_send()
        for level in range(levels):
            reduce_copy(level, j).wait_send()
            gather_copy(level, j).wait_send()


def body(spectra, source_block, taper_window):
    f_all, parts, shot_dev, node_dev = spectra.shape
    nodes = lax.axis_size("node")
    groups = lax.axis_size("shot")
    levels = nodes.bit_length() - 1
    rounds = source_block.shape[0]
    f_dev = f_all // groups
    shots = shot_dev * groups
    rows = rounds * SB
    fs = max(2, nodes // 8)
    stages = f_dev // fs
    unit = fs * parts * rows // nodes
    scale = 1.0 / float(shots) ** 0.5

    first = lax.axis_index("node") * node_dev
    picked = source_block[:, None] * SB + jnp.arange(SB, dtype=jnp.int32)[None, :] - first
    sel = (picked.reshape(rows, 1) == jnp.arange(node_dev, dtype=jnp.int32)[None, :]).astype(jnp.bfloat16)
    weights = taper_weights(taper_window)

    bf = jnp.bfloat16
    dma = pltpu.SemaphoreType.DMA
    return pl.pallas_call(
        functools.partial(kernel, nodes, groups, stages, scale),
        out_shape=jax.ShapeDtypeStruct((rounds, f_dev, parts, SB, node_dev), bf),
        in_specs=[
            pl.BlockSpec(memory_space=pltpu.VMEM),
            pl.BlockSpec(memory_space=pltpu.VMEM),
            pl.BlockSpec(memory_space=pl.ANY),
        ],
        out_specs=pl.BlockSpec(memory_space=pltpu.VMEM),
        scratch_shapes=[
            pltpu.VMEM((f_dev, parts, groups, shot_dev, node_dev), bf),
            pltpu.VMEM((stages, nodes, unit, shots), bf),
            pltpu.VMEM((stages, nodes, unit, shots), bf),
            *[pltpu.VMEM((stages, nodes >> (level + 1), unit, shots), bf) for level in range(levels)],
            dma,
            dma((stages, groups - 1)),
            dma((stages, groups - 1)),
            dma((levels, stages)),
            dma((levels, stages)),
            dma((levels, stages)),
            dma((levels, stages)),
        ],
        compiler_params=pltpu.CompilerParams(
            collective_id=0, has_side_effects=True, vmem_limit_bytes=48 * 1024 * 1024
        ),
        cost_estimate=pl.CostEstimate(
            flops=2 * 5 * f_dev * rows * shots * node_dev * 2, bytes_accessed=spectra.size * 4, transcendentals=0
        ),
    )(sel, weights, spectra)


def solution(mesh):
    in_specs = (P(None, None, "shot", "node"), P(), P())
    out_specs = P(None, "shot", None, None, "node")
    return jax.shard_map(body, mesh=mesh, in_specs=in_specs, out_specs=out_specs, check_vma=False)
```

```python
import functools

import jax
import jax.numpy as jnp
from jax import lax
from jax.experimental import pallas as pl
from jax.experimental.pallas import tpu as pltpu
from jax.sharding import PartitionSpec as P

SB = 32
WINDOWS = 8
MESH = pl.DeviceIdType.MESH
AHEAD = 4


def taper_weights(taper_windows):
    return 0.5 - 0.5 * jnp.cos(jnp.pi * (taper_windows.astype(jnp.float32) + 1.0) / (WINDOWS + 1.0))


def kernel(
    nodes, groups, stages, scale,
    sel_ref, weight_ref, x_ref, out_ref,
    recv, part, full, *rest,
):
    levels = nodes.bit_length() - 1
    land = rest[:levels]
    own_sem, zs, zr, rs, rr, gs, gr = rest[levels:]
    me = lax.axis_index("node")
    group = lax.axis_index("shot")
    f_dev = recv.shape[0]
    fs = f_dev // stages
    rows = sel_ref.shape[0]
    shots = part.shape[-1]
    unit = part.shape[2]
    per = rows // unit
    rounds = rows // SB
    receivers = recv.shape[-1]

    def peer_at(stride):
        bit = (me // stride) % 2
        return bit, me + stride * (1 - 2 * bit)

    def hop(level, j):
        bit, peer = peer_at(2**level)
        if level:
            bit_odd, peer_odd = peer_at(2 ** (levels - level))
            odd = j % 2
            bit = bit + odd * (bit_odd - bit)
            peer = peer + odd * (peer_odd - peer)
        return bit, peer

    def offset(level, j):
        at = 0
        for lower in range(level):
            at = at + hop(lower, j)[0] * (nodes >> (lower + 1))
        return at

    def spectra_copy(j, d):
        to = (group + d) % groups
        return pltpu.make_async_remote_copy(
            src_ref=x_ref.at[pl.ds(to * f_dev + j * fs, fs)],
            dst_ref=recv.at[pl.ds(j * fs, fs), :, group],
            send_sem=zs.at[j, d - 1],
            recv_sem=zr.at[j, d - 1],
            device_id=(me, to),
            device_id_type=MESH,
        )

    def spectra_arrival(j, d):
        source = (group + groups - d) % groups
        place = recv.at[pl.ds(j * fs, fs), :, source]
        return pltpu.make_async_remote_copy(
            src_ref=place,
            dst_ref=place,
            send_sem=zs.at[j, d - 1],
            recv_sem=zr.at[j, d - 1],
            device_id=(me, source),
            device_id_type=MESH,
        )

    def reduce_copy(level, j):
        bit, peer = hop(level, j)
        size = nodes >> (level + 1)
        return pltpu.make_async_remote_copy(
            src_ref=part.at[j, pl.ds(offset(level, j) + (1 - bit) * size, size)],
            dst_ref=land[level].at[j],
            send_sem=rs.at[level, j],
            recv_sem=rr.at[level, j],
            device_id=(peer, group),
            device_id_type=MESH,
        )

    def gather_copy(level, j, arrival=False):
        bit, peer = hop(level, j)
        size = nodes >> (level + 1)
        half = 1 - bit if arrival else bit
        place = full.at[j, pl.ds(offset(level, j) + half * size, size)]
        return pltpu.make_async_remote_copy(
            src_ref=place,
            dst_ref=place,
            send_sem=gs.at[level, j],
            recv_sem=gr.at[level, j],
            device_id=(peer, group),
            device_id_type=MESH,
        )

    own_copy = pltpu.make_async_copy(
        x_ref.at[pl.ds(group * f_dev, f_dev)], recv.at[:, :, group], own_sem
    )
    own_copy.start()

    barrier = pltpu.get_barrier_semaphore()
    for level in range(levels):
        pl.semaphore_signal(barrier, inc=1, device_id=(peer_at(2**level)[1], group), device_id_type=MESH)
    for d in range(1, groups):
        pl.semaphore_signal(barrier, inc=1, device_id=(me, (group + d) % groups), device_id_type=MESH)
    pl.semaphore_wait(barrier, levels + groups - 1)

    def send_spectra(j):
        for d in range(1, groups):
            spectra_copy(j, d).start()

    for j in range(min(AHEAD, stages)):
        send_spectra(j)
    own_copy.wait()

    def select(j):
        for d in range(1, groups):
            spectra_arrival(j, d).wait_recv()

        @pl.when(j + AHEAD < stages)
        def _():
            send_spectra(j + AHEAD)

        for f in range(fs):
            for c in range(2):
                block = recv[j * fs + f, c].reshape(shots, receivers)
                picked = lax.dot_general(
                    sel_ref[...], block, (((1,), (1,)), ((), ())),
                    preferred_element_type=jnp.float32,
                ).reshape(rounds, SB, shots)
                tapered = (picked * weight_ref[...][:, None, :]).astype(jnp.bfloat16)
                part[j, pl.ds((f * 2 + c) * per, per)] = tapered.reshape(per, unit, shots)
        reduce_copy(0, j).start()

    def reduce(level, j):
        reduce_copy(level, j).wait_recv()
        bit, _ = hop(level, j)
        size = nodes >> (level + 1)
        kept = pl.ds(offset(level, j) + bit * size, size)
        total = part[j, kept] + land[level][j]
        if level + 1 < levels:
            part[j, kept] = total
            reduce_copy(level + 1, j).start()
        else:
            full[j, kept] = total
            gather_copy(level, j).start()

    def correlate(j):
        for f in range(fs):
            first = full[j, pl.ds(2 * f * per, per)].reshape(rows, shots)
            second = full[j, pl.ds((2 * f + 1) * per, per)].reshape(rows, shots)
            both = jnp.concatenate(
                [recv[j * fs + f, c].reshape(shots, receivers) for c in range(2)], axis=1
            )
            by_first = jnp.dot(first, both, preferred_element_type=jnp.float32)
            by_second = jnp.dot(second, both, preferred_element_type=jnp.float32)
            real = (by_first[:, :receivers] + by_second[:, receivers:]) * scale
            imag = (by_first[:, receivers:] - by_second[:, :receivers]) * scale
            out_ref[:, j * fs + f, 0] = real.reshape(rounds, SB, receivers).astype(jnp.bfloat16)
            out_ref[:, j * fs + f, 1] = imag.reshape(rounds, SB, receivers).astype(jnp.bfloat16)

    def gather(level, j):
        gather_copy(level, j, arrival=True).wait_recv()
        if level:
            gather_copy(level - 1, j).start()
        else:
            correlate(j)

    steps = [select]
    steps += [functools.partial(reduce, level) for level in range(levels)]
    steps += [functools.partial(gather, level) for level in reversed(range(levels))]

    @pl.loop(0, stages + len(steps) - 1)
    def _(tick):
        for place in reversed(range(len(steps))):
            j = tick - place
            pl.when((j >= 0) & (j < stages))(functools.partial(steps[place], j))

    @pl.loop(0, stages)
    def _(j):
        for d in range(1, groups):
            spectra_copy(j, d).wait_send()
        for level in range(levels):
            reduce_copy(level, j).wait_send()
            gather_copy(level, j).wait_send()


def body(spectra, source_block, taper_window):
    f_all, parts, shot_dev, node_dev = spectra.shape
    nodes = lax.axis_size("node")
    groups = lax.axis_size("shot")
    levels = nodes.bit_length() - 1
    rounds = source_block.shape[0]
    f_dev = f_all // groups
    shots = shot_dev * groups
    rows = rounds * SB
    fs = max(1, nodes // 8)
    stages = f_dev // fs
    unit = fs * parts * rows // nodes
    scale = 1.0 / float(shots) ** 0.5

    first = lax.axis_index("node") * node_dev
    picked = source_block[:, None] * SB + jnp.arange(SB, dtype=jnp.int32)[None, :] - first
    sel = (picked.reshape(rows, 1) == jnp.arange(node_dev, dtype=jnp.int32)[None, :]).astype(jnp.bfloat16)
    weights = taper_weights(taper_window)

    bf = jnp.bfloat16
    dma = pltpu.SemaphoreType.DMA
    return pl.pallas_call(
        functools.partial(kernel, nodes, groups, stages, scale),
        out_shape=jax.ShapeDtypeStruct((rounds, f_dev, parts, SB, node_dev), bf),
        in_specs=[
            pl.BlockSpec(memory_space=pltpu.VMEM),
            pl.BlockSpec(memory_space=pltpu.VMEM),
            pl.BlockSpec(memory_space=pl.ANY),
        ],
        out_specs=pl.BlockSpec(memory_space=pltpu.VMEM),
        scratch_shapes=[
            pltpu.VMEM((f_dev, parts, groups, shot_dev, node_dev), bf),
            pltpu.VMEM((stages, nodes, unit, shots), bf),
            pltpu.VMEM((stages, nodes, unit, shots), bf),
            *[pltpu.VMEM((stages, nodes >> (level + 1), unit, shots), bf) for level in range(levels)],
            dma,
            dma((stages, groups - 1)),
            dma((stages, groups - 1)),
            dma((levels, stages)),
            dma((levels, stages)),
            dma((levels, stages)),
            dma((levels, stages)),
        ],
        compiler_params=pltpu.CompilerParams(
            collective_id=0, has_side_effects=True, vmem_limit_bytes=60 * 1024 * 1024
        ),
        cost_estimate=pl.CostEstimate(
            flops=2 * 5 * f_dev * rows * shots * node_dev * 2, bytes_accessed=spectra.size * 4, transcendentals=0
        ),
    )(sel, weights, spectra)


def solution(mesh):
    in_specs = (P(None, None, "shot", "node"), P(), P())
    out_specs = P(None, "shot", None, None, "node")
    return jax.shard_map(body, mesh=mesh, in_specs=in_specs, out_specs=out_specs, check_vma=False)
```

```python
import functools

import jax
import jax.numpy as jnp
from jax import lax
from jax.experimental import pallas as pl
from jax.experimental.pallas import tpu as pltpu
from jax.sharding import PartitionSpec as P

SB = 32
WINDOWS = 8
MESH = pl.DeviceIdType.MESH
AHEAD = 4
SPACING = 2


def taper_weights(taper_windows):
    return 0.5 - 0.5 * jnp.cos(jnp.pi * (taper_windows.astype(jnp.float32) + 1.0) / (WINDOWS + 1.0))


def kernel(
    nodes, groups, stages, scale,
    sel_ref, weight_ref, x_ref, out_ref,
    recv, part, full, *rest,
):
    levels = nodes.bit_length() - 1
    land = rest[:levels]
    own_sem, zs, zr, rs, rr, gs, gr = rest[levels:]
    me = lax.axis_index("node")
    group = lax.axis_index("shot")
    f_dev = recv.shape[0]
    fs = f_dev // stages
    rows = sel_ref.shape[0]
    shots = part.shape[-1]
    unit = part.shape[2]
    per = rows // unit
    rounds = rows // SB
    receivers = recv.shape[-1]

    def peer_at(stride):
        bit = (me // stride) % 2
        return bit, me + stride * (1 - 2 * bit)

    def hop(level, j):
        bit, peer = peer_at(2**level)
        if level:
            bit_odd, peer_odd = peer_at(2 ** (levels - level))
            odd = j % 2
            bit = bit + odd * (bit_odd - bit)
            peer = peer + odd * (peer_odd - peer)
        return bit, peer

    def offset(level, j):
        at = 0
        for lower in range(level):
            at = at + hop(lower, j)[0] * (nodes >> (lower + 1))
        return at

    def spectra_copy(j, d):
        to = (group + d) % groups
        return pltpu.make_async_remote_copy(
            src_ref=x_ref.at[pl.ds(to * f_dev + j * fs, fs)],
            dst_ref=recv.at[pl.ds(j * fs, fs), :, group],
            send_sem=zs.at[j, d - 1],
            recv_sem=zr.at[j, d - 1],
            device_id=(me, to),
            device_id_type=MESH,
        )

    def spectra_arrival(j, d):
        source = (group + groups - d) % groups
        place = recv.at[pl.ds(j * fs, fs), :, source]
        return pltpu.make_async_remote_copy(
            src_ref=place,
            dst_ref=place,
            send_sem=zs.at[j, d - 1],
            recv_sem=zr.at[j, d - 1],
            device_id=(me, source),
            device_id_type=MESH,
        )

    def reduce_copy(level, j):
        bit, peer = hop(level, j)
        size = nodes >> (level + 1)
        return pltpu.make_async_remote_copy(
            src_ref=part.at[j, pl.ds(offset(level, j) + (1 - bit) * size, size)],
            dst_ref=land[level].at[j],
            send_sem=rs.at[level, j],
            recv_sem=rr.at[level, j],
            device_id=(peer, group),
            device_id_type=MESH,
        )

    def gather_copy(level, j, arrival=False):
        bit, peer = hop(level, j)
        size = nodes >> (level + 1)
        half = 1 - bit if arrival else bit
        place = full.at[j, pl.ds(offset(level, j) + half * size, size)]
        return pltpu.make_async_remote_copy(
            src_ref=place,
            dst_ref=place,
            send_sem=gs.at[level, j],
            recv_sem=gr.at[level, j],
            device_id=(peer, group),
            device_id_type=MESH,
        )

    own_copy = pltpu.make_async_copy(
        x_ref.at[pl.ds(group * f_dev, f_dev)], recv.at[:, :, group], own_sem
    )
    own_copy.start()

    barrier = pltpu.get_barrier_semaphore()
    for level in range(levels):
        pl.semaphore_signal(barrier, inc=1, device_id=(peer_at(2**level)[1], group), device_id_type=MESH)
    for d in range(1, groups):
        pl.semaphore_signal(barrier, inc=1, device_id=(me, (group + d) % groups), device_id_type=MESH)
    pl.semaphore_wait(barrier, levels + groups - 1)

    def send_spectra(j):
        for d in range(1, groups):
            spectra_copy(j, d).start()

    for j in range(min(AHEAD, stages)):
        send_spectra(j)
    own_copy.wait()

    def select(j):
        for d in range(1, groups):
            spectra_arrival(j, d).wait_recv()

        @pl.when(j + AHEAD < stages)
        def _():
            send_spectra(j + AHEAD)

        for f in range(fs):
            for c in range(2):
                block = recv[j * fs + f, c].reshape(shots, receivers)
                picked = lax.dot_general(
                    sel_ref[...], block, (((1,), (1,)), ((), ())),
                    preferred_element_type=jnp.float32,
                ).reshape(rounds, SB, shots)
                tapered = (picked * weight_ref[...][:, None, :]).astype(jnp.bfloat16)
                part[j, pl.ds((f * 2 + c) * per, per)] = tapered.reshape(per, unit, shots)
        reduce_copy(0, j).start()

    def reduce(level, j):
        reduce_copy(level, j).wait_recv()
        bit, _ = hop(level, j)
        size = nodes >> (level + 1)
        kept = pl.ds(offset(level, j) + bit * size, size)
        total = part[j, kept] + land[level][j]
        if level + 1 < levels:
            part[j, kept] = total
            reduce_copy(level + 1, j).start()
        else:
            full[j, kept] = total
            gather_copy(level, j).start()

    def correlate(j):
        for f in range(fs):
            first = full[j, pl.ds(2 * f * per, per)].reshape(rows, shots)
            second = full[j, pl.ds((2 * f + 1) * per, per)].reshape(rows, shots)
            both = jnp.concatenate(
                [recv[j * fs + f, c].reshape(shots, receivers) for c in range(2)], axis=1
            )
            by_first = jnp.dot(first, both, preferred_element_type=jnp.float32)
            by_second = jnp.dot(second, both, preferred_element_type=jnp.float32)
            real = (by_first[:, :receivers] + by_second[:, receivers:]) * scale
            imag = (by_first[:, receivers:] - by_second[:, :receivers]) * scale
            out_ref[:, j * fs + f, 0] = real.reshape(rounds, SB, receivers).astype(jnp.bfloat16)
            out_ref[:, j * fs + f, 1] = imag.reshape(rounds, SB, receivers).astype(jnp.bfloat16)

    def gather(level, j):
        gather_copy(level, j, arrival=True).wait_recv()
        if level:
            gather_copy(level - 1, j).start()
        else:
            correlate(j)

    steps = [select]
    steps += [functools.partial(reduce, level) for level in range(levels)]
    steps += [functools.partial(gather, level) for level in reversed(range(levels))]

    @pl.loop(0, stages + SPACING * (len(steps) - 1))
    def _(tick):
        for place in reversed(range(len(steps))):
            j = tick - SPACING * place
            pl.when((j >= 0) & (j < stages))(functools.partial(steps[place], j))

    @pl.loop(0, stages)
    def _(j):
        for d in range(1, groups):
            spectra_copy(j, d).wait_send()
        for level in range(levels):
            reduce_copy(level, j).wait_send()
            gather_copy(level, j).wait_send()


def body(spectra, source_block, taper_window):
    f_all, parts, shot_dev, node_dev = spectra.shape
    nodes = lax.axis_size("node")
    groups = lax.axis_size("shot")
    levels = nodes.bit_length() - 1
    rounds = source_block.shape[0]
    f_dev = f_all // groups
    shots = shot_dev * groups
    rows = rounds * SB
    fs = max(1, nodes // 8)
    stages = f_dev // fs
    unit = fs * parts * rows // nodes
    scale = 1.0 / float(shots) ** 0.5

    first = lax.axis_index("node") * node_dev
    picked = source_block[:, None] * SB + jnp.arange(SB, dtype=jnp.int32)[None, :] - first
    sel = (picked.reshape(rows, 1) == jnp.arange(node_dev, dtype=jnp.int32)[None, :]).astype(jnp.bfloat16)
    weights = taper_weights(taper_window)

    bf = jnp.bfloat16
    dma = pltpu.SemaphoreType.DMA
    return pl.pallas_call(
        functools.partial(kernel, nodes, groups, stages, scale),
        out_shape=jax.ShapeDtypeStruct((rounds, f_dev, parts, SB, node_dev), bf),
        in_specs=[
            pl.BlockSpec(memory_space=pltpu.VMEM),
            pl.BlockSpec(memory_space=pltpu.VMEM),
            pl.BlockSpec(memory_space=pl.ANY),
        ],
        out_specs=pl.BlockSpec(memory_space=pltpu.VMEM),
        scratch_shapes=[
            pltpu.VMEM((f_dev, parts, groups, shot_dev, node_dev), bf),
            pltpu.VMEM((stages, nodes, unit, shots), bf),
            pltpu.VMEM((stages, nodes, unit, shots), bf),
            *[pltpu.VMEM((stages, nodes >> (level + 1), unit, shots), bf) for level in range(levels)],
            dma,
            dma((stages, groups - 1)),
            dma((stages, groups - 1)),
            dma((levels, stages)),
            dma((levels, stages)),
            dma((levels, stages)),
            dma((levels, stages)),
        ],
        compiler_params=pltpu.CompilerParams(
            collective_id=0, has_side_effects=True, vmem_limit_bytes=48 * 1024 * 1024
        ),
        cost_estimate=pl.CostEstimate(
            flops=2 * 5 * f_dev * rows * shots * node_dev * 2, bytes_accessed=spectra.size * 4, transcendentals=0
        ),
    )(sel, weights, spectra)


def solution(mesh):
    in_specs = (P(None, None, "shot", "node"), P(), P())
    out_specs = P(None, "shot", None, None, "node")
    return jax.shard_map(body, mesh=mesh, in_specs=in_specs, out_specs=out_specs, check_vma=False)
```

```python
import functools

import jax
import jax.numpy as jnp
from jax import lax
from jax.experimental import pallas as pl
from jax.experimental.pallas import tpu as pltpu
from jax.sharding import PartitionSpec as P

SB = 32
WINDOWS = 8
MESH = pl.DeviceIdType.MESH
AHEAD = 6
SPACING = 2
LATER = 5


def taper_weights(taper_windows):
    return 0.5 - 0.5 * jnp.cos(jnp.pi * (taper_windows.astype(jnp.float32) + 1.0) / (WINDOWS + 1.0))


def kernel(
    nodes, groups, stages, scale,
    sel_ref, weight_ref, x_ref, out_ref,
    recv, part, full, acc, out_part, in_part, *rest,
):
    levels = nodes.bit_length() - 1
    land = rest[:levels]
    own_sem, zs, zr, rs, rr, gs, gr, ps, pr = rest[levels:]
    me = lax.axis_index("node")
    group = lax.axis_index("shot")
    half = groups // 2
    side, rank = group // half, group % half
    counterpart = (1 - side) * half + rank
    fs = recv.shape[1]
    f_dev = stages * fs
    halves = stages // 2
    mid = part.shape[-1] // 2
    rows = sel_ref.shape[0]
    shots = part.shape[-1]
    unit = part.shape[2]
    per = rows // unit
    rounds = rows // SB
    receivers = recv.shape[-1]

    def peer_at(stride):
        bit = (me // stride) % 2
        return bit, me + stride * (1 - 2 * bit)

    def hop(level, j):
        bit, peer = peer_at(2**level)
        if level:
            bit_odd, peer_odd = peer_at(2 ** (levels - level))
            odd = j % 2
            bit = bit + odd * (bit_odd - bit)
            peer = peer + odd * (peer_odd - peer)
        return bit, peer

    def offset(level, j):
        at = 0
        for lower in range(level):
            at = at + hop(lower, j)[0] * (nodes >> (lower + 1))
        return at

    def is_split(j):
        return (j == 0) | ((j % 2 == 1) & (j < stages - 1))

    def split_first(j):
        return (j + 1) // 2 * fs

    def whole_first(j):
        return (halves + (j + 1) // 2 - 1) * fs

    def frequencies(owner, first):
        return x_ref.at[pl.ds(owner * f_dev + first, fs)]

    def send(j, number, source, slot, to):
        return pltpu.make_async_remote_copy(
            src_ref=source,
            dst_ref=recv.at[j, :, :, slot],
            send_sem=zs.at[j, number],
            recv_sem=zr.at[j, number],
            device_id=(me, to),
            device_id_type=MESH,
        )

    def whole_sends(j):
        first = whole_first(j)
        out = []
        for d in range(1, groups):
            to = (group + d) % groups
            out.append(send(j, d - 1, frequencies(to, first), group, to))
        return out

    def whole_arrivals(j):
        out = []
        for d in range(1, groups):
            source = (group + groups - d) % groups
            out.append(send(j, d - 1, recv.at[j, :, :, source], source, source))
        return out

    def split_sends(j):
        first = split_first(j)
        out = []
        for d in range(1, half):
            to = (rank + d) % half
            for other in range(2):
                owner = (side + other * (1 - 2 * side)) * half + to
                out.append(
                    send(j, 2 * (d - 1) + other, frequencies(owner, first), other * half + rank, side * half + to)
                )
        return out

    def split_arrivals(j):
        out = []
        for d in range(1, half):
            source = (rank + half - d) % half
            for other in range(2):
                place = other * half + source
                out.append(send(j, 2 * (d - 1) + other, recv.at[j, :, :, place], place, side * half + source))
        return out

    def whole_own(j):
        return [
            pltpu.make_async_copy(frequencies(group, whole_first(j)), recv.at[j, :, :, group], own_sem.at[j, 0])
        ]

    def split_own(j):
        return [
            pltpu.make_async_copy(frequencies(group, split_first(j)), recv.at[j, :, :, rank], own_sem.at[j, 0]),
            pltpu.make_async_copy(
                frequencies(counterpart, split_first(j)), recv.at[j, :, :, half + rank], own_sem.at[j, 1]
            ),
        ]

    def partial_copy(j):
        place = pl.ds(split_first(j), fs)
        return pltpu.make_async_remote_copy(
            src_ref=out_part.at[place],
            dst_ref=in_part.at[place],
            send_sem=ps.at[j],
            recv_sem=pr.at[j],
            device_id=(me, counterpart),
            device_id_type=MESH,
        )

    def by_kind(j, on_split, on_whole):
        split = is_split(j)
        pl.when(split)(functools.partial(on_split, j))
        pl.when(jnp.logical_not(split))(functools.partial(on_whole, j))

    def reduce_copy(level, j):
        bit, peer = hop(level, j)
        size = nodes >> (level + 1)
        return pltpu.make_async_remote_copy(
            src_ref=part.at[j, pl.ds(offset(level, j) + (1 - bit) * size, size)],
            dst_ref=land[level].at[j],
            send_sem=rs.at[level, j],
            recv_sem=rr.at[level, j],
            device_id=(peer, group),
            device_id_type=MESH,
        )

    def gather_copy(level, j, arrival=False):
        bit, peer = hop(level, j)
        size = nodes >> (level + 1)
        side_at = 1 - bit if arrival else bit
        place = full.at[j, pl.ds(offset(level, j) + side_at * size, size)]
        return pltpu.make_async_remote_copy(
            src_ref=place,
            dst_ref=place,
            send_sem=gs.at[level, j],
            recv_sem=gr.at[level, j],
            device_id=(peer, group),
            device_id_type=MESH,
        )

    barrier = pltpu.get_barrier_semaphore()
    for level in range(levels):
        pl.semaphore_signal(barrier, inc=1, device_id=(peer_at(2**level)[1], group), device_id_type=MESH)
    for d in range(1, groups):
        pl.semaphore_signal(barrier, inc=1, device_id=(me, (group + d) % groups), device_id_type=MESH)
    pl.semaphore_wait(barrier, levels + groups - 1)

    def start_split(j):
        for copy in split_sends(j) + split_own(j):
            copy.start()

    def start_whole(j):
        for copy in whole_sends(j) + whole_own(j):
            copy.start()

    @pl.loop(0, min(AHEAD, stages))
    def _(j):
        by_kind(j, start_split, start_whole)

    def pick(j, kind):
        for f in range(fs):
            for c in range(2):
                block = recv[j, f, c].reshape(shots, receivers)
                picked = lax.dot_general(
                    sel_ref[...], block, (((1,), (1,)), ((), ())),
                    preferred_element_type=jnp.float32,
                ).reshape(rounds, SB, shots)
                tapered = (picked * weight_ref[kind][:, None, :]).astype(jnp.bfloat16)
                part[j, pl.ds((f * 2 + c) * per, per)] = tapered.reshape(per, unit, shots)

    def select_split(j):
        for copy in split_own(j):
            copy.wait()
        for copy in split_arrivals(j):
            copy.wait_recv()
        pick(j, 1)

    def select_whole(j):
        for copy in whole_own(j):
            copy.wait()
        for copy in whole_arrivals(j):
            copy.wait_recv()
        pick(j, 0)

    def select(j):
        pl.when(j + AHEAD < stages)(lambda: by_kind(j + AHEAD, start_split, start_whole))
        by_kind(j, select_split, select_whole)
        reduce_copy(0, j).start()

    def reduce(level, j):
        reduce_copy(level, j).wait_recv()
        bit, _ = hop(level, j)
        size = nodes >> (level + 1)
        kept = pl.ds(offset(level, j) + bit * size, size)
        total = part[j, kept] + land[level][j]
        if level + 1 < levels:
            part[j, kept] = total
            reduce_copy(level + 1, j).start()
        else:
            full[j, kept] = total
            gather_copy(level, j).start()

    def products(j, f, shots_at):
        first = full[j, pl.ds(2 * f * per, per)].reshape(rows, shots)[:, shots_at]
        second = full[j, pl.ds((2 * f + 1) * per, per)].reshape(rows, shots)[:, shots_at]
        both = jnp.concatenate(
            [recv[j, f, c].reshape(shots, receivers)[shots_at] for c in range(2)], axis=1
        )
        by_first = jnp.dot(first, both, preferred_element_type=jnp.float32)
        by_second = jnp.dot(second, both, preferred_element_type=jnp.float32)
        real = by_first[:, :receivers] + by_second[:, receivers:]
        imag = by_first[:, receivers:] - by_second[:, :receivers]
        return real, imag

    def store(at, pair):
        for c in range(2):
            out_ref[:, at, c] = (pair[c] * scale).reshape(rounds, SB, receivers).astype(jnp.bfloat16)

    def correlate_whole(j):
        for f in range(fs):
            store(whole_first(j) + f, products(j, f, slice(None)))

    def correlate_split(j):
        for f in range(fs):
            at = split_first(j) + f
            pair = products(j, f, slice(mid, None))
            for c in range(2):
                out_part[at, c] = pair[c].astype(jnp.bfloat16)
        partial_copy(j).start()
        for f in range(fs):
            at = split_first(j) + f
            pair = products(j, f, slice(0, mid))
            for c in range(2):
                acc[at, c] = pair[c]

    def correlate(j):
        by_kind(j, correlate_split, correlate_whole)

    def combine(j):
        partial_copy(j).wait_recv()
        for f in range(fs):
            at = split_first(j) + f
            store(at, [acc[at, c] + in_part[at, c].astype(jnp.float32) for c in range(2)])

    def gather(level, j):
        gather_copy(level, j, arrival=True).wait_recv()
        if level:
            gather_copy(level - 1, j).start()
        else:
            correlate(j)

    steps = [select]
    steps += [functools.partial(reduce, level) for level in range(levels)]
    steps += [functools.partial(gather, level) for level in reversed(range(levels))]

    last = SPACING * (len(steps) - 1) + LATER

    @pl.loop(0, stages + last)
    def _(tick):
        for place in reversed(range(len(steps))):
            j = tick - SPACING * place
            pl.when((j >= 0) & (j < stages))(functools.partial(steps[place], j))
        j = tick - last
        pl.when((j >= 0) & (j < stages) & is_split(j))(functools.partial(combine, j))

    def sent_split(j):
        for copy in split_sends(j) + [partial_copy(j)]:
            copy.wait_send()

    def sent_whole(j):
        for copy in whole_sends(j):
            copy.wait_send()

    @pl.loop(0, stages)
    def _(j):
        by_kind(j, sent_split, sent_whole)
        for level in range(levels):
            reduce_copy(level, j).wait_send()
            gather_copy(level, j).wait_send()


def body(spectra, source_block, taper_window):
    f_all, parts, shot_dev, node_dev = spectra.shape
    nodes = lax.axis_size("node")
    groups = lax.axis_size("shot")
    levels = nodes.bit_length() - 1
    rounds = source_block.shape[0]
    f_dev = f_all // groups
    shots = shot_dev * groups
    rows = rounds * SB
    fs = max(1, nodes // 8)
    stages = f_dev // fs
    unit = fs * parts * rows // nodes
    scale = 1.0 / float(shots) ** 0.5

    first = lax.axis_index("node") * node_dev
    picked = source_block[:, None] * SB + jnp.arange(SB, dtype=jnp.int32)[None, :] - first
    sel = (picked.reshape(rows, 1) == jnp.arange(node_dev, dtype=jnp.int32)[None, :]).astype(jnp.bfloat16)
    weights = taper_weights(taper_window)
    here = lax.axis_index("shot") // (groups // 2) * (shots // 2)
    weights_here = lax.dynamic_slice_in_dim(weights, here, shots // 2, 1)
    weights = jnp.stack((weights, jnp.concatenate((weights_here, weights_here), axis=1)))

    bf = jnp.bfloat16
    dma = pltpu.SemaphoreType.DMA
    return pl.pallas_call(
        functools.partial(kernel, nodes, groups, stages, scale),
        out_shape=jax.ShapeDtypeStruct((rounds, f_dev, parts, SB, node_dev), bf),
        in_specs=[
            pl.BlockSpec(memory_space=pltpu.VMEM),
            pl.BlockSpec(memory_space=pltpu.VMEM),
            pl.BlockSpec(memory_space=pl.ANY),
        ],
        out_specs=pl.BlockSpec(memory_space=pltpu.VMEM),
        scratch_shapes=[
            pltpu.VMEM((stages, fs, parts, groups, shot_dev, node_dev), bf),
            pltpu.VMEM((stages, nodes, unit, shots), bf),
            pltpu.VMEM((stages, nodes, unit, shots), bf),
            pltpu.VMEM((f_dev // 2, parts, rows, node_dev), jnp.float32),
            pltpu.VMEM((f_dev // 2, parts, rows, node_dev), bf),
            pltpu.VMEM((f_dev // 2, parts, rows, node_dev), bf),
            *[pltpu.VMEM((stages, nodes >> (level + 1), unit, shots), bf) for level in range(levels)],
            dma((stages, 2)),
            dma((stages, groups - 1)),
            dma((stages, groups - 1)),
            dma((levels, stages)),
            dma((levels, stages)),
            dma((levels, stages)),
            dma((levels, stages)),
            dma((stages,)),
            dma((stages,)),
        ],
        compiler_params=pltpu.CompilerParams(
            collective_id=0, has_side_effects=True, vmem_limit_bytes=48 * 1024 * 1024
        ),
        cost_estimate=pl.CostEstimate(
            flops=2 * 5 * f_dev * rows * shots * node_dev * 2, bytes_accessed=spectra.size * 4, transcendentals=0
        ),
    )(sel, weights, spectra)


def solution(mesh):
    in_specs = (P(None, None, "shot", "node"), P(), P())
    out_specs = P(None, "shot", None, None, "node")
    return jax.shard_map(body, mesh=mesh, in_specs=in_specs, out_specs=out_specs, check_vma=False)
```

```python
import functools

import jax
import jax.numpy as jnp
from jax import lax
from jax.experimental import pallas as pl
from jax.experimental.pallas import tpu as pltpu
from jax.sharding import PartitionSpec as P

SB = 32
WINDOWS = 8
MESH = pl.DeviceIdType.MESH
AHEAD = 16
SPACING = 2
LATER = 5


def taper_weights(taper_windows):
    return 0.5 - 0.5 * jnp.cos(jnp.pi * (taper_windows.astype(jnp.float32) + 1.0) / (WINDOWS + 1.0))


def kernel(
    nodes, groups, stages, scale,
    block_ref, window_ref, x_ref, out_ref,
    sel_ref, weight_ref, recv, part, full, acc, out_part, in_part, *rest,
):
    levels = nodes.bit_length() - 1
    land = rest[:levels]
    own_sem, zs, zr, rs, rr, gs, gr, ps, pr = rest[levels:]
    me = lax.axis_index("node")
    group = lax.axis_index("shot")
    half = groups // 2
    side, rank = group // half, group % half
    counterpart = (1 - side) * half + rank
    fs = recv.shape[1]
    f_dev = stages * fs
    halves = stages // 2
    mid = part.shape[-1] // 2
    rows = sel_ref.shape[0]
    shots = part.shape[-1]
    unit = part.shape[2]
    per = rows // unit
    rounds = rows // SB
    receivers = recv.shape[-1]

    def peer_at(stride):
        bit = (me // stride) % 2
        return bit, me + stride * (1 - 2 * bit)

    def hop(level, j):
        bit, peer = peer_at(2**level)
        if level:
            bit_odd, peer_odd = peer_at(2 ** (levels - level))
            odd = j % 2
            bit = bit + odd * (bit_odd - bit)
            peer = peer + odd * (peer_odd - peer)
        return bit, peer

    def offset(level, j):
        at = 0
        for lower in range(level):
            at = at + hop(lower, j)[0] * (nodes >> (lower + 1))
        return at

    def is_split(j):
        return (j == 0) | ((j % 2 == 1) & (j < stages - 1))

    def split_first(j):
        return (j + 1) // 2 * fs

    def whole_first(j):
        return (halves + (j + 1) // 2 - 1) * fs

    def frequencies(owner, first):
        return x_ref.at[pl.ds(owner * f_dev + first, fs)]

    def send(j, number, source, slot, to):
        return pltpu.make_async_remote_copy(
            src_ref=source,
            dst_ref=recv.at[j, :, :, slot],
            send_sem=zs.at[j, number],
            recv_sem=zr.at[j, number],
            device_id=(me, to),
            device_id_type=MESH,
        )

    def whole_sends(j):
        first = whole_first(j)
        out = []
        for d in range(1, groups):
            to = (group + d) % groups
            out.append(send(j, d - 1, frequencies(to, first), group, to))
        return out

    def whole_arrivals(j):
        out = []
        for d in range(1, groups):
            source = (group + groups - d) % groups
            out.append(send(j, d - 1, recv.at[j, :, :, source], source, source))
        return out

    def split_sends(j):
        first = split_first(j)
        out = []
        for d in range(1, half):
            to = (rank + d) % half
            for other in range(2):
                owner = (side + other * (1 - 2 * side)) * half + to
                out.append(
                    send(j, 2 * (d - 1) + other, frequencies(owner, first), other * half + rank, side * half + to)
                )
        return out

    def split_arrivals(j):
        out = []
        for d in range(1, half):
            source = (rank + half - d) % half
            for other in range(2):
                place = other * half + source
                out.append(send(j, 2 * (d - 1) + other, recv.at[j, :, :, place], place, side * half + source))
        return out

    def whole_own(j):
        return [
            pltpu.make_async_copy(frequencies(group, whole_first(j)), recv.at[j, :, :, group], own_sem.at[j, 0])
        ]

    def split_own(j):
        return [
            pltpu.make_async_copy(frequencies(group, split_first(j)), recv.at[j, :, :, rank], own_sem.at[j, 0]),
            pltpu.make_async_copy(
                frequencies(counterpart, split_first(j)), recv.at[j, :, :, half + rank], own_sem.at[j, 1]
            ),
        ]

    def partial_copy(j):
        place = pl.ds(split_first(j), fs)
        return pltpu.make_async_remote_copy(
            src_ref=out_part.at[place],
            dst_ref=in_part.at[place],
            send_sem=ps.at[j],
            recv_sem=pr.at[j],
            device_id=(me, counterpart),
            device_id_type=MESH,
        )

    def by_kind(j, on_split, on_whole):
        split = is_split(j)
        pl.when(split)(functools.partial(on_split, j))
        pl.when(jnp.logical_not(split))(functools.partial(on_whole, j))

    def reduce_copy(level, j):
        bit, peer = hop(level, j)
        size = nodes >> (level + 1)
        return pltpu.make_async_remote_copy(
            src_ref=part.at[j, pl.ds(offset(level, j) + (1 - bit) * size, size)],
            dst_ref=land[level].at[j],
            send_sem=rs.at[level, j],
            recv_sem=rr.at[level, j],
            device_id=(peer, group),
            device_id_type=MESH,
        )

    def gather_copy(level, j, arrival=False):
        bit, peer = hop(level, j)
        size = nodes >> (level + 1)
        side_at = 1 - bit if arrival else bit
        place = full.at[j, pl.ds(offset(level, j) + side_at * size, size)]
        return pltpu.make_async_remote_copy(
            src_ref=place,
            dst_ref=place,
            send_sem=gs.at[level, j],
            recv_sem=gr.at[level, j],
            device_id=(peer, group),
            device_id_type=MESH,
        )

    barrier = pltpu.get_barrier_semaphore()
    for level in range(levels):
        pl.semaphore_signal(barrier, inc=1, device_id=(peer_at(2**level)[1], group), device_id_type=MESH)
    for d in range(1, groups):
        pl.semaphore_signal(barrier, inc=1, device_id=(me, (group + d) % groups), device_id_type=MESH)
    pl.semaphore_wait(barrier, levels + groups - 1)

    def start_split(j):
        for copy in split_sends(j) + split_own(j):
            copy.start()

    def start_whole(j):
        for copy in whole_sends(j) + whole_own(j):
            copy.start()

    @pl.loop(0, min(AHEAD, stages))
    def _(j):
        by_kind(j, start_split, start_whole)

    for r in range(rounds):
        at = block_ref[r] * SB - me * receivers
        column = lax.broadcasted_iota(jnp.int32, (SB, receivers), 1)
        row = lax.broadcasted_iota(jnp.int32, (SB, receivers), 0)
        sel_ref[pl.ds(r * SB, SB)] = jnp.where(column == row + at, 1.0, 0.0).astype(jnp.bfloat16)
    weights = taper_weights(window_ref[...])
    low, high = weights[:, :mid], weights[:, mid:]
    here = jnp.where(side == 0, low, high)
    weight_ref[0] = weights
    weight_ref[1] = jnp.concatenate((here, here), axis=1)

    def pick(j, kind):
        for f in range(fs):
            for c in range(2):
                block = recv[j, f, c].reshape(shots, receivers)
                picked = lax.dot_general(
                    sel_ref[...], block, (((1,), (1,)), ((), ())),
                    preferred_element_type=jnp.float32,
                ).reshape(rounds, SB, shots)
                tapered = (picked * weight_ref[kind][:, None, :]).astype(jnp.bfloat16)
                part[j, pl.ds((f * 2 + c) * per, per)] = tapered.reshape(per, unit, shots)

    def select_split(j):
        for copy in split_own(j):
            copy.wait()
        for copy in split_arrivals(j):
            copy.wait_recv()
        pick(j, 1)

    def select_whole(j):
        for copy in whole_own(j):
            copy.wait()
        for copy in whole_arrivals(j):
            copy.wait_recv()
        pick(j, 0)

    def select(j):
        pl.when(j + AHEAD < stages)(lambda: by_kind(j + AHEAD, start_split, start_whole))
        by_kind(j, select_split, select_whole)
        reduce_copy(0, j).start()

    def reduce(level, j):
        reduce_copy(level, j).wait_recv()
        bit, _ = hop(level, j)
        size = nodes >> (level + 1)
        kept = pl.ds(offset(level, j) + bit * size, size)
        total = part[j, kept] + land[level][j]
        if level + 1 < levels:
            part[j, kept] = total
            reduce_copy(level + 1, j).start()
        else:
            full[j, kept] = total
            gather_copy(level, j).start()

    def products(j, f, shots_at):
        first = full[j, pl.ds(2 * f * per, per)].reshape(rows, shots)[:, shots_at]
        second = full[j, pl.ds((2 * f + 1) * per, per)].reshape(rows, shots)[:, shots_at]
        both = jnp.concatenate(
            [recv[j, f, c].reshape(shots, receivers)[shots_at] for c in range(2)], axis=1
        )
        by_first = jnp.dot(first, both, preferred_element_type=jnp.float32)
        by_second = jnp.dot(second, both, preferred_element_type=jnp.float32)
        real = by_first[:, :receivers] + by_second[:, receivers:]
        imag = by_first[:, receivers:] - by_second[:, :receivers]
        return real, imag

    def store(at, pair):
        for c in range(2):
            out_ref[:, at, c] = (pair[c] * scale).reshape(rounds, SB, receivers).astype(jnp.bfloat16)

    def correlate_whole(j):
        for f in range(fs):
            store(whole_first(j) + f, products(j, f, slice(None)))

    def correlate_split(j):
        for f in range(fs):
            at = split_first(j) + f
            pair = products(j, f, slice(mid, None))
            for c in range(2):
                out_part[at, c] = pair[c].astype(jnp.bfloat16)
        partial_copy(j).start()
        for f in range(fs):
            at = split_first(j) + f
            pair = products(j, f, slice(0, mid))
            for c in range(2):
                acc[at, c] = pair[c]

    def correlate(j):
        by_kind(j, correlate_split, correlate_whole)

    def combine(j):
        partial_copy(j).wait_recv()
        for f in range(fs):
            at = split_first(j) + f
            store(at, [acc[at, c] + in_part[at, c].astype(jnp.float32) for c in range(2)])

    def gather(level, j):
        gather_copy(level, j, arrival=True).wait_recv()
        if level:
            gather_copy(level - 1, j).start()
        else:
            correlate(j)

    steps = [select]
    steps += [functools.partial(reduce, level) for level in range(levels)]
    steps += [functools.partial(gather, level) for level in reversed(range(levels))]

    last = SPACING * (len(steps) - 1) + LATER

    @pl.loop(0, stages + last)
    def _(tick):
        for place in reversed(range(len(steps))):
            j = tick - SPACING * place
            pl.when((j >= 0) & (j < stages))(functools.partial(steps[place], j))
        j = tick - last
        pl.when((j >= 0) & (j < stages) & is_split(j))(functools.partial(combine, j))

    def sent_split(j):
        for copy in split_sends(j) + [partial_copy(j)]:
            copy.wait_send()

    def sent_whole(j):
        for copy in whole_sends(j):
            copy.wait_send()

    @pl.loop(0, stages)
    def _(j):
        by_kind(j, sent_split, sent_whole)
        for level in range(levels):
            reduce_copy(level, j).wait_send()
            gather_copy(level, j).wait_send()


def body(spectra, source_block, taper_window):
    f_all, parts, shot_dev, node_dev = spectra.shape
    nodes = lax.axis_size("node")
    groups = lax.axis_size("shot")
    levels = nodes.bit_length() - 1
    rounds = source_block.shape[0]
    f_dev = f_all // groups
    shots = shot_dev * groups
    rows = rounds * SB
    fs = max(1, nodes // 8)
    stages = f_dev // fs
    unit = fs * parts * rows // nodes
    scale = 1.0 / float(shots) ** 0.5

    bf = jnp.bfloat16
    dma = pltpu.SemaphoreType.DMA
    return pl.pallas_call(
        functools.partial(kernel, nodes, groups, stages, scale),
        out_shape=jax.ShapeDtypeStruct((rounds, f_dev, parts, SB, node_dev), bf),
        in_specs=[
            pl.BlockSpec(memory_space=pltpu.SMEM),
            pl.BlockSpec(memory_space=pltpu.VMEM),
            pl.BlockSpec(memory_space=pl.ANY),
        ],
        out_specs=pl.BlockSpec(memory_space=pltpu.VMEM),
        scratch_shapes=[
            pltpu.VMEM((rows, node_dev), bf),
            pltpu.VMEM((2, rounds, shots), jnp.float32),
            pltpu.VMEM((stages, fs, parts, groups, shot_dev, node_dev), bf),
            pltpu.VMEM((stages, nodes, unit, shots), bf),
            pltpu.VMEM((stages, nodes, unit, shots), bf),
            pltpu.VMEM((f_dev // 2, parts, rows, node_dev), jnp.float32),
            pltpu.VMEM((f_dev // 2, parts, rows, node_dev), bf),
            pltpu.VMEM((f_dev // 2, parts, rows, node_dev), bf),
            *[pltpu.VMEM((stages, nodes >> (level + 1), unit, shots), bf) for level in range(levels)],
            dma((stages, 2)),
            dma((stages, groups - 1)),
            dma((stages, groups - 1)),
            dma((levels, stages)),
            dma((levels, stages)),
            dma((levels, stages)),
            dma((levels, stages)),
            dma((stages,)),
            dma((stages,)),
        ],
        compiler_params=pltpu.CompilerParams(
            collective_id=0, has_side_effects=True, vmem_limit_bytes=51 * 1024 * 1024
        ),
        cost_estimate=pl.CostEstimate(
            flops=2 * 5 * f_dev * rows * shots * node_dev * 2, bytes_accessed=spectra.size * 4, transcendentals=0
        ),
    )(source_block, taper_window, spectra)


def solution(mesh):
    in_specs = (P(None, None, "shot", "node"), P(), P())
    out_specs = P(None, "shot", None, None, "node")
    return jax.shard_map(body, mesh=mesh, in_specs=in_specs, out_specs=out_specs, check_vma=False)
```

```python
import functools

import jax
import jax.numpy as jnp
from jax import lax
from jax.experimental import pallas as pl
from jax.experimental.pallas import tpu as pltpu
from jax.sharding import PartitionSpec as P

SB = 32
WINDOWS = 8
MESH = pl.DeviceIdType.MESH
AHEAD = 16
SPACING = 2
LATER = 9


def taper_weights(taper_windows):
    return 0.5 - 0.5 * jnp.cos(jnp.pi * (taper_windows.astype(jnp.float32) + 1.0) / (WINDOWS + 1.0))


def kernel(
    nodes, groups, stages, scale,
    block_ref, window_ref, x_ref, out_ref,
    sel_ref, weight_ref, recv, part, full, acc, out_part, in_part, *rest,
):
    levels = nodes.bit_length() - 1
    land = rest[:levels]
    own_sem, zs, zr, rs, rr, gs, gr, ps, pr = rest[levels:]
    me = lax.axis_index("node")
    group = lax.axis_index("shot")
    half = groups // 2
    side, rank = group // half, group % half
    counterpart = (1 - side) * half + rank
    fs = recv.shape[1]
    f_dev = stages * fs
    halves = stages // 2
    mid = part.shape[-1] // 2
    rows = sel_ref.shape[0]
    shots = part.shape[-1]
    unit = part.shape[2]
    per = rows // unit
    rounds = rows // SB
    receivers = recv.shape[-1]

    def peer_at(stride):
        bit = (me // stride) % 2
        return bit, me + stride * (1 - 2 * bit)

    def hop(level, j):
        bit, peer = peer_at(2**level)
        if level:
            bit_odd, peer_odd = peer_at(2 ** (levels - level))
            odd = j % 2
            bit = bit + odd * (bit_odd - bit)
            peer = peer + odd * (peer_odd - peer)
        return bit, peer

    def offset(level, j):
        at = 0
        for lower in range(level):
            at = at + hop(lower, j)[0] * (nodes >> (lower + 1))
        return at

    def is_split(j):
        return (j == 0) | ((j % 2 == 1) & (j < stages - 1))

    def split_first(j):
        return (j + 1) // 2 * fs

    def whole_first(j):
        return (halves + (j + 1) // 2 - 1) * fs

    def frequencies(owner, first):
        return x_ref.at[pl.ds(owner * f_dev + first, fs)]

    def send(j, number, source, slot, to):
        return pltpu.make_async_remote_copy(
            src_ref=source,
            dst_ref=recv.at[j, :, :, slot],
            send_sem=zs.at[j, number],
            recv_sem=zr.at[j, number],
            device_id=(me, to),
            device_id_type=MESH,
        )

    def whole_sends(j):
        first = whole_first(j)
        out = []
        for d in range(1, groups):
            to = (group + d) % groups
            out.append(send(j, d - 1, frequencies(to, first), group, to))
        return out

    def whole_arrivals(j):
        out = []
        for d in range(1, groups):
            source = (group + groups - d) % groups
            out.append(send(j, d - 1, recv.at[j, :, :, source], source, source))
        return out

    def split_sends(j):
        first = split_first(j)
        out = []
        for d in range(1, half):
            to = (rank + d) % half
            for other in range(2):
                owner = (side + other * (1 - 2 * side)) * half + to
                out.append(
                    send(j, 2 * (d - 1) + other, frequencies(owner, first), other * half + rank, side * half + to)
                )
        return out

    def split_arrivals(j):
        out = []
        for d in range(1, half):
            source = (rank + half - d) % half
            for other in range(2):
                place = other * half + source
                out.append(send(j, 2 * (d - 1) + other, recv.at[j, :, :, place], place, side * half + source))
        return out

    def whole_own(j):
        return [
            pltpu.make_async_copy(frequencies(group, whole_first(j)), recv.at[j, :, :, group], own_sem.at[j, 0])
        ]

    def split_own(j):
        return [
            pltpu.make_async_copy(frequencies(group, split_first(j)), recv.at[j, :, :, rank], own_sem.at[j, 0]),
            pltpu.make_async_copy(
                frequencies(counterpart, split_first(j)), recv.at[j, :, :, half + rank], own_sem.at[j, 1]
            ),
        ]

    def partial_copy(j):
        place = pl.ds(split_first(j), fs)
        return pltpu.make_async_remote_copy(
            src_ref=out_part.at[place],
            dst_ref=in_part.at[place],
            send_sem=ps.at[j],
            recv_sem=pr.at[j],
            device_id=(me, counterpart),
            device_id_type=MESH,
        )

    def by_kind(j, on_split, on_whole):
        split = is_split(j)
        pl.when(split)(functools.partial(on_split, j))
        pl.when(jnp.logical_not(split))(functools.partial(on_whole, j))

    def reduce_copy(level, j):
        bit, peer = hop(level, j)
        size = nodes >> (level + 1)
        return pltpu.make_async_remote_copy(
            src_ref=part.at[j, pl.ds(offset(level, j) + (1 - bit) * size, size)],
            dst_ref=land[level].at[j],
            send_sem=rs.at[level, j],
            recv_sem=rr.at[level, j],
            device_id=(peer, group),
            device_id_type=MESH,
        )

    def gather_copy(level, j, arrival=False):
        bit, peer = hop(level, j)
        size = nodes >> (level + 1)
        side_at = 1 - bit if arrival else bit
        place = full.at[j, pl.ds(offset(level, j) + side_at * size, size)]
        return pltpu.make_async_remote_copy(
            src_ref=place,
            dst_ref=place,
            send_sem=gs.at[level, j],
            recv_sem=gr.at[level, j],
            device_id=(peer, group),
            device_id_type=MESH,
        )

    barrier = pltpu.get_barrier_semaphore()
    for level in range(levels):
        pl.semaphore_signal(barrier, inc=1, device_id=(peer_at(2**level)[1], group), device_id_type=MESH)
    for d in range(1, groups):
        pl.semaphore_signal(barrier, inc=1, device_id=(me, (group + d) % groups), device_id_type=MESH)
    pl.semaphore_wait(barrier, levels + groups - 1)

    def start_split(j):
        for copy in split_sends(j) + split_own(j):
            copy.start()

    def start_whole(j):
        for copy in whole_sends(j) + whole_own(j):
            copy.start()

    @pl.loop(0, min(AHEAD, stages))
    def _(j):
        by_kind(j, start_split, start_whole)

    for r in range(rounds):
        at = block_ref[r] * SB - me * receivers
        column = lax.broadcasted_iota(jnp.int32, (SB, receivers), 1)
        row = lax.broadcasted_iota(jnp.int32, (SB, receivers), 0)
        sel_ref[pl.ds(r * SB, SB)] = jnp.where(column == row + at, 1.0, 0.0).astype(jnp.bfloat16)
    weights = taper_weights(window_ref[...])
    low, high = weights[:, :mid], weights[:, mid:]
    here = jnp.where(side == 0, low, high)
    weight_ref[0] = weights
    weight_ref[1] = jnp.concatenate((here, here), axis=1)

    def pick(j, kind):
        for f in range(fs):
            for c in range(2):
                block = recv[j, f, c].reshape(shots, receivers)
                picked = lax.dot_general(
                    sel_ref[...], block, (((1,), (1,)), ((), ())),
                    preferred_element_type=jnp.float32,
                ).reshape(rounds, SB, shots)
                tapered = (picked * weight_ref[kind][:, None, :]).astype(jnp.bfloat16)
                part[j, pl.ds((f * 2 + c) * per, per)] = tapered.reshape(per, unit, shots)

    def select_split(j):
        for copy in split_own(j):
            copy.wait()
        for copy in split_arrivals(j):
            copy.wait_recv()
        pick(j, 1)

    def select_whole(j):
        for copy in whole_own(j):
            copy.wait()
        for copy in whole_arrivals(j):
            copy.wait_recv()
        pick(j, 0)

    def select(j):
        pl.when(j + AHEAD < stages)(lambda: by_kind(j + AHEAD, start_split, start_whole))
        by_kind(j, select_split, select_whole)
        reduce_copy(0, j).start()

    def reduce(level, j):
        reduce_copy(level, j).wait_recv()
        bit, _ = hop(level, j)
        size = nodes >> (level + 1)
        kept = pl.ds(offset(level, j) + bit * size, size)
        total = part[j, kept] + land[level][j]
        if level + 1 < levels:
            part[j, kept] = total
            reduce_copy(level + 1, j).start()
        else:
            full[j, kept] = total
            gather_copy(level, j).start()

    def products(j, f, shots_at):
        first = full[j, pl.ds(2 * f * per, per)].reshape(rows, shots)[:, shots_at]
        second = full[j, pl.ds((2 * f + 1) * per, per)].reshape(rows, shots)[:, shots_at]
        both = jnp.concatenate(
            [recv[j, f, c].reshape(shots, receivers)[shots_at] for c in range(2)], axis=1
        )
        by_first = jnp.dot(first, both, preferred_element_type=jnp.float32)
        by_second = jnp.dot(second, both, preferred_element_type=jnp.float32)
        real = by_first[:, :receivers] + by_second[:, receivers:]
        imag = by_first[:, receivers:] - by_second[:, :receivers]
        return real, imag

    def store(at, pair):
        for c in range(2):
            out_ref[:, at, c] = (pair[c] * scale).reshape(rounds, SB, receivers).astype(jnp.bfloat16)

    def correlate_whole(j):
        for f in range(fs):
            store(whole_first(j) + f, products(j, f, slice(None)))

    def correlate_split(j):
        for f in range(fs):
            at = split_first(j) + f
            pair = products(j, f, slice(mid, None))
            for c in range(2):
                out_part[at, c] = pair[c].astype(jnp.bfloat16)
        partial_copy(j).start()
        for f in range(fs):
            at = split_first(j) + f
            pair = products(j, f, slice(0, mid))
            for c in range(2):
                acc[at, c] = pair[c]

    def correlate(j):
        by_kind(j, correlate_split, correlate_whole)

    def combine(j):
        partial_copy(j).wait_recv()
        for f in range(fs):
            at = split_first(j) + f
            store(at, [acc[at, c] + in_part[at, c].astype(jnp.float32) for c in range(2)])

    def gather(level, j):
        gather_copy(level, j, arrival=True).wait_recv()
        if level:
            gather_copy(level - 1, j).start()
        else:
            correlate(j)

    steps = [select]
    steps += [functools.partial(reduce, level) for level in range(levels)]
    steps += [functools.partial(gather, level) for level in reversed(range(levels))]

    last = SPACING * (len(steps) - 1) + LATER

    @pl.loop(0, stages + last)
    def _(tick):
        for place in [*reversed(range(1, len(steps) - 1)), len(steps) - 1, 0]:
            j = tick - SPACING * place
            pl.when((j >= 0) & (j < stages))(functools.partial(steps[place], j))
        j = tick - last
        pl.when((j >= 0) & (j < stages) & is_split(j))(functools.partial(combine, j))

    def sent_split(j):
        for copy in split_sends(j) + [partial_copy(j)]:
            copy.wait_send()

    def sent_whole(j):
        for copy in whole_sends(j):
            copy.wait_send()

    @pl.loop(0, stages)
    def _(j):
        by_kind(j, sent_split, sent_whole)
        for level in range(levels):
            reduce_copy(level, j).wait_send()
            gather_copy(level, j).wait_send()


def body(spectra, source_block, taper_window):
    f_all, parts, shot_dev, node_dev = spectra.shape
    nodes = lax.axis_size("node")
    groups = lax.axis_size("shot")
    levels = nodes.bit_length() - 1
    rounds = source_block.shape[0]
    f_dev = f_all // groups
    shots = shot_dev * groups
    rows = rounds * SB
    fs = max(1, nodes // 8)
    stages = f_dev // fs
    unit = fs * parts * rows // nodes
    scale = 1.0 / float(shots) ** 0.5

    bf = jnp.bfloat16
    dma = pltpu.SemaphoreType.DMA
    return pl.pallas_call(
        functools.partial(kernel, nodes, groups, stages, scale),
        out_shape=jax.ShapeDtypeStruct((rounds, f_dev, parts, SB, node_dev), bf),
        in_specs=[
            pl.BlockSpec(memory_space=pltpu.SMEM),
            pl.BlockSpec(memory_space=pltpu.VMEM),
            pl.BlockSpec(memory_space=pl.ANY),
        ],
        out_specs=pl.BlockSpec(memory_space=pltpu.VMEM),
        scratch_shapes=[
            pltpu.VMEM((rows, node_dev), bf),
            pltpu.VMEM((2, rounds, shots), jnp.float32),
            pltpu.VMEM((stages, fs, parts, groups, shot_dev, node_dev), bf),
            pltpu.VMEM((stages, nodes, unit, shots), bf),
            pltpu.VMEM((stages, nodes, unit, shots), bf),
            pltpu.VMEM((f_dev // 2, parts, rows, node_dev), jnp.float32),
            pltpu.VMEM((f_dev // 2, parts, rows, node_dev), bf),
            pltpu.VMEM((f_dev // 2, parts, rows, node_dev), bf),
            *[pltpu.VMEM((stages, nodes >> (level + 1), unit, shots), bf) for level in range(levels)],
            dma((stages, 2)),
            dma((stages, groups - 1)),
            dma((stages, groups - 1)),
            dma((levels, stages)),
            dma((levels, stages)),
            dma((levels, stages)),
            dma((levels, stages)),
            dma((stages,)),
            dma((stages,)),
        ],
        compiler_params=pltpu.CompilerParams(
            collective_id=0, has_side_effects=True, vmem_limit_bytes=51 * 1024 * 1024
        ),
        cost_estimate=pl.CostEstimate(
            flops=2 * 5 * f_dev * rows * shots * node_dev * 2, bytes_accessed=spectra.size * 4, transcendentals=0
        ),
    )(source_block, taper_window, spectra)


def solution(mesh):
    in_specs = (P(None, None, "shot", "node"), P(), P())
    out_specs = P(None, "shot", None, None, "node")
    return jax.shard_map(body, mesh=mesh, in_specs=in_specs, out_specs=out_specs, check_vma=False)
```

```python
import functools

import jax
import jax.numpy as jnp
from jax import lax
from jax.experimental import pallas as pl
from jax.experimental.pallas import tpu as pltpu
from jax.sharding import PartitionSpec as P

SB = 32
WINDOWS = 8
MESH = pl.DeviceIdType.MESH
AHEAD = 16
SPACING = 2
LATER = 9


def taper_weights(taper_windows):
    return 0.5 - 0.5 * jnp.cos(jnp.pi * (taper_windows.astype(jnp.float32) + 1.0) / (WINDOWS + 1.0))


def kernel(
    nodes, groups, stages, scale,
    block_ref, window_ref, x_ref, out_ref,
    sel_ref, weight_ref, recv, part, full, acc, out_part, in_part, *rest,
):
    levels = nodes.bit_length() - 1
    land = rest[:levels]
    own_sem, zs, zr, rs, rr, gs, gr, ps, pr = rest[levels:]
    me = lax.axis_index("node")
    group = lax.axis_index("shot")
    half = groups // 2
    side, rank = group // half, group % half
    counterpart = (1 - side) * half + rank
    fs = recv.shape[2]
    f_dev = stages * fs
    splits = acc.shape[0] // fs
    wholes = stages - splits
    mid = part.shape[-1] // 2
    rows = sel_ref.shape[0]
    shots = part.shape[-1]
    unit = part.shape[2]
    per = rows // unit
    rounds = rows // SB
    receivers = recv.shape[-1]

    def peer_at(stride):
        bit = (me // stride) % 2
        return bit, me + stride * (1 - 2 * bit)

    def hop(level, j):
        bit, peer = peer_at(2**level)
        if level:
            bit_odd, peer_odd = peer_at(2 ** (levels - level))
            odd = j % 2
            bit = bit + odd * (bit_odd - bit)
            peer = peer + odd * (peer_odd - peer)
        return bit, peer

    def offset(level, j):
        at = 0
        for lower in range(level):
            at = at + hop(lower, j)[0] * (nodes >> (lower + 1))
        return at

    def wholes_before(j):
        return j * (wholes - 1) // (stages - 1)

    def is_split(j):
        return (j < stages - 1) & (wholes_before(j + 1) == wholes_before(j))

    def split_first(j):
        return (j - wholes_before(j)) * fs

    def whole_first(j):
        return (splits + wholes_before(j)) * fs

    def frequencies(owner, first):
        return x_ref.at[pl.ds(owner * f_dev + first, fs)]

    def send(j, number, source, slot, to):
        return pltpu.make_async_remote_copy(
            src_ref=source,
            dst_ref=recv.at[j, slot],
            send_sem=zs.at[j, number],
            recv_sem=zr.at[j, number],
            device_id=(me, to),
            device_id_type=MESH,
        )

    def whole_sends(j):
        first = whole_first(j)
        out = []
        for d in range(1, groups):
            to = (group + d) % groups
            out.append(send(j, d - 1, frequencies(to, first), group, to))
        return out

    def whole_arrivals(j):
        out = []
        for d in range(1, groups):
            source = (group + groups - d) % groups
            out.append(send(j, d - 1, recv.at[j, source], source, source))
        return out

    def split_sends(j):
        first = split_first(j)
        out = []
        for d in range(1, half):
            to = (rank + d) % half
            for other in range(2):
                owner = (side + other * (1 - 2 * side)) * half + to
                out.append(
                    send(j, 2 * (d - 1) + other, frequencies(owner, first), other * half + rank, side * half + to)
                )
        return out

    def split_arrivals(j):
        out = []
        for d in range(1, half):
            source = (rank + half - d) % half
            for other in range(2):
                place = other * half + source
                out.append(send(j, 2 * (d - 1) + other, recv.at[j, place], place, side * half + source))
        return out

    def whole_own(j):
        return [
            pltpu.make_async_copy(frequencies(group, whole_first(j)), recv.at[j, group], own_sem.at[j, 0])
        ]

    def split_own(j):
        return [
            pltpu.make_async_copy(frequencies(group, split_first(j)), recv.at[j, rank], own_sem.at[j, 0]),
            pltpu.make_async_copy(
                frequencies(counterpart, split_first(j)), recv.at[j, half + rank], own_sem.at[j, 1]
            ),
        ]

    def partial_copy(j):
        place = pl.ds(split_first(j), fs)
        return pltpu.make_async_remote_copy(
            src_ref=out_part.at[place],
            dst_ref=in_part.at[place],
            send_sem=ps.at[j],
            recv_sem=pr.at[j],
            device_id=(me, counterpart),
            device_id_type=MESH,
        )

    def by_kind(j, on_split, on_whole):
        split = is_split(j)
        pl.when(split)(functools.partial(on_split, j))
        pl.when(jnp.logical_not(split))(functools.partial(on_whole, j))

    def reduce_copy(level, j):
        bit, peer = hop(level, j)
        size = nodes >> (level + 1)
        return pltpu.make_async_remote_copy(
            src_ref=part.at[j, pl.ds(offset(level, j) + (1 - bit) * size, size)],
            dst_ref=land[level].at[j],
            send_sem=rs.at[level, j],
            recv_sem=rr.at[level, j],
            device_id=(peer, group),
            device_id_type=MESH,
        )

    def gather_copy(level, j, arrival=False):
        bit, peer = hop(level, j)
        size = nodes >> (level + 1)
        side_at = 1 - bit if arrival else bit
        place = full.at[j, pl.ds(offset(level, j) + side_at * size, size)]
        return pltpu.make_async_remote_copy(
            src_ref=place,
            dst_ref=place,
            send_sem=gs.at[level, j],
            recv_sem=gr.at[level, j],
            device_id=(peer, group),
            device_id_type=MESH,
        )

    barrier = pltpu.get_barrier_semaphore()
    for level in range(levels):
        pl.semaphore_signal(barrier, inc=1, device_id=(peer_at(2**level)[1], group), device_id_type=MESH)
    for d in range(1, groups):
        pl.semaphore_signal(barrier, inc=1, device_id=(me, (group + d) % groups), device_id_type=MESH)
    pl.semaphore_wait(barrier, levels + groups - 1)

    def start_split(j):
        for copy in split_sends(j) + split_own(j):
            copy.start()

    def start_whole(j):
        for copy in whole_sends(j) + whole_own(j):
            copy.start()

    @pl.loop(0, min(AHEAD, stages))
    def _(j):
        by_kind(j, start_split, start_whole)

    for r in range(rounds):
        at = block_ref[r] * SB - me * receivers
        column = lax.broadcasted_iota(jnp.int32, (SB, receivers), 1)
        row = lax.broadcasted_iota(jnp.int32, (SB, receivers), 0)
        sel_ref[pl.ds(r * SB, SB)] = jnp.where(column == row + at, 1.0, 0.0).astype(jnp.bfloat16)
    weights = taper_weights(window_ref[...])
    low, high = weights[:, :mid], weights[:, mid:]
    here = jnp.where(side == 0, low, high)
    weight_ref[0] = weights
    weight_ref[1] = jnp.concatenate((here, here), axis=1)

    def pick(j, kind):
        for f in range(fs):
            for c in range(2):
                block = recv[j, :, f, c].reshape(shots, receivers)
                picked = lax.dot_general(
                    sel_ref[...], block, (((1,), (1,)), ((), ())),
                    preferred_element_type=jnp.float32,
                ).reshape(rounds, SB, shots)
                tapered = (picked * weight_ref[kind][:, None, :]).astype(jnp.bfloat16)
                part[j, pl.ds((f * 2 + c) * per, per)] = tapered.reshape(per, unit, shots)

    def select_split(j):
        for copy in split_own(j):
            copy.wait()
        for copy in split_arrivals(j):
            copy.wait_recv()
        pick(j, 1)

    def select_whole(j):
        for copy in whole_own(j):
            copy.wait()
        for copy in whole_arrivals(j):
            copy.wait_recv()
        pick(j, 0)

    def select(j):
        pl.when(j + AHEAD < stages)(lambda: by_kind(j + AHEAD, start_split, start_whole))
        by_kind(j, select_split, select_whole)
        reduce_copy(0, j).start()

    def reduce(level, j):
        reduce_copy(level, j).wait_recv()
        bit, _ = hop(level, j)
        size = nodes >> (level + 1)
        kept = pl.ds(offset(level, j) + bit * size, size)
        total = part[j, kept] + land[level][j]
        if level + 1 < levels:
            part[j, kept] = total
            reduce_copy(level + 1, j).start()
        else:
            full[j, kept] = total
            gather_copy(level, j).start()

    def products(j, f, shots_at):
        first = full[j, pl.ds(2 * f * per, per)].reshape(rows, shots)[:, shots_at]
        second = full[j, pl.ds((2 * f + 1) * per, per)].reshape(rows, shots)[:, shots_at]
        both = jnp.concatenate(
            [recv[j, :, f, c].reshape(shots, receivers)[shots_at] for c in range(2)], axis=1
        )
        by_first = jnp.dot(first, both, preferred_element_type=jnp.float32)
        by_second = jnp.dot(second, both, preferred_element_type=jnp.float32)
        real = by_first[:, :receivers] + by_second[:, receivers:]
        imag = by_first[:, receivers:] - by_second[:, :receivers]
        return real, imag

    def store(at, pair):
        for c in range(2):
            out_ref[:, at, c] = (pair[c] * scale).reshape(rounds, SB, receivers).astype(jnp.bfloat16)

    def correlate_whole(j):
        for f in range(fs):
            store(whole_first(j) + f, products(j, f, slice(None)))

    def correlate_split(j):
        for f in range(fs):
            at = split_first(j) + f
            pair = products(j, f, slice(mid, None))
            for c in range(2):
                out_part[at, c] = pair[c].astype(jnp.bfloat16)
        partial_copy(j).start()
        for f in range(fs):
            at = split_first(j) + f
            pair = products(j, f, slice(0, mid))
            for c in range(2):
                acc[at, c] = pair[c]

    def correlate(j):
        by_kind(j, correlate_split, correlate_whole)

    def combine(j):
        partial_copy(j).wait_recv()
        for f in range(fs):
            at = split_first(j) + f
            store(at, [acc[at, c] + in_part[at, c].astype(jnp.float32) for c in range(2)])

    def gather(level, j):
        gather_copy(level, j, arrival=True).wait_recv()
        if level:
            gather_copy(level - 1, j).start()
        else:
            correlate(j)

    steps = [select]
    steps += [functools.partial(reduce, level) for level in range(levels)]
    steps += [functools.partial(gather, level) for level in reversed(range(levels))]

    last = SPACING * (len(steps) - 1) + LATER

    @pl.loop(0, stages + last)
    def _(tick):
        for place in [*reversed(range(1, len(steps) - 1)), len(steps) - 1, 0]:
            j = tick - SPACING * place
            pl.when((j >= 0) & (j < stages))(functools.partial(steps[place], j))
        j = tick - last
        pl.when((j >= 0) & (j < stages) & is_split(j))(functools.partial(combine, j))

    def sent_split(j):
        for copy in split_sends(j) + [partial_copy(j)]:
            copy.wait_send()

    def sent_whole(j):
        for copy in whole_sends(j):
            copy.wait_send()

    @pl.loop(0, stages)
    def _(j):
        by_kind(j, sent_split, sent_whole)
        for level in range(levels):
            reduce_copy(level, j).wait_send()
            gather_copy(level, j).wait_send()


def body(spectra, source_block, taper_window):
    f_all, parts, shot_dev, node_dev = spectra.shape
    nodes = lax.axis_size("node")
    groups = lax.axis_size("shot")
    levels = nodes.bit_length() - 1
    rounds = source_block.shape[0]
    f_dev = f_all // groups
    shots = shot_dev * groups
    rows = rounds * SB
    fs = max(1, nodes // 8)
    stages = f_dev // fs
    splits = max(1, stages * 5 // 8)
    unit = fs * parts * rows // nodes
    scale = 1.0 / float(shots) ** 0.5

    bf = jnp.bfloat16
    dma = pltpu.SemaphoreType.DMA
    return pl.pallas_call(
        functools.partial(kernel, nodes, groups, stages, scale),
        out_shape=jax.ShapeDtypeStruct((rounds, f_dev, parts, SB, node_dev), bf),
        in_specs=[
            pl.BlockSpec(memory_space=pltpu.SMEM),
            pl.BlockSpec(memory_space=pltpu.VMEM),
            pl.BlockSpec(memory_space=pl.ANY),
        ],
        out_specs=pl.BlockSpec(memory_space=pltpu.VMEM),
        scratch_shapes=[
            pltpu.VMEM((rows, node_dev), bf),
            pltpu.VMEM((2, rounds, shots), jnp.float32),
            pltpu.VMEM((stages, groups, fs, parts, shot_dev, node_dev), bf),
            pltpu.VMEM((stages, nodes, unit, shots), bf),
            pltpu.VMEM((stages, nodes, unit, shots), bf),
            pltpu.VMEM((splits * fs, parts, rows, node_dev), jnp.float32),
            pltpu.VMEM((splits * fs, parts, rows, node_dev), bf),
            pltpu.VMEM((splits * fs, parts, rows, node_dev), bf),
            *[pltpu.VMEM((stages, nodes >> (level + 1), unit, shots), bf) for level in range(levels)],
            dma((stages, 2)),
            dma((stages, groups - 1)),
            dma((stages, groups - 1)),
            dma((levels, stages)),
            dma((levels, stages)),
            dma((levels, stages)),
            dma((levels, stages)),
            dma((stages,)),
            dma((stages,)),
        ],
        compiler_params=pltpu.CompilerParams(
            collective_id=0, has_side_effects=True, vmem_limit_bytes=51 * 1024 * 1024
        ),
        cost_estimate=pl.CostEstimate(
            flops=2 * 5 * f_dev * rows * shots * node_dev * 2, bytes_accessed=spectra.size * 4, transcendentals=0
        ),
    )(source_block, taper_window, spectra)


def solution(mesh):
    in_specs = (P(None, None, "shot", "node"), P(), P())
    out_specs = P(None, "shot", None, None, "node")
    return jax.shard_map(body, mesh=mesh, in_specs=in_specs, out_specs=out_specs, check_vma=False)
```

```python
import functools

import jax
import jax.numpy as jnp
from jax import lax
from jax.experimental import pallas as pl
from jax.experimental.pallas import tpu as pltpu
from jax.sharding import PartitionSpec as P

SB = 32
WINDOWS = 8
MESH = pl.DeviceIdType.MESH
AHEAD = 16
SPACING = 3
LATER = 6


def taper_weights(taper_windows):
    return 0.5 - 0.5 * jnp.cos(jnp.pi * (taper_windows.astype(jnp.float32) + 1.0) / (WINDOWS + 1.0))


def kernel(
    nodes, groups, stages, scale,
    block_ref, window_ref, x_ref, out_ref,
    sel_ref, weight_ref, recv, part, full, acc, out_part, in_part, *rest,
):
    levels = nodes.bit_length() - 1
    land = rest[:levels]
    own_sem, zs, zr, rs, rr, gs, gr, ps, pr = rest[levels:]
    me = lax.axis_index("node")
    group = lax.axis_index("shot")
    half = groups // 2
    side, rank = group // half, group % half
    counterpart = (1 - side) * half + rank
    fs = recv.shape[2]
    f_dev = stages * fs
    splits = acc.shape[0] // fs
    wholes = stages - splits
    mid = part.shape[-1] // 2
    rows = sel_ref.shape[0]
    shots = part.shape[-1]
    unit = part.shape[2]
    per = rows // unit
    rounds = rows // SB
    receivers = recv.shape[-1]

    def peer_at(stride):
        bit = (me // stride) % 2
        return bit, me + stride * (1 - 2 * bit)

    def hop(level, j):
        bit, peer = peer_at(2**level)
        if level:
            bit_odd, peer_odd = peer_at(2 ** (levels - level))
            odd = j % 2
            bit = bit + odd * (bit_odd - bit)
            peer = peer + odd * (peer_odd - peer)
        return bit, peer

    def offset(level, j):
        at = 0
        for lower in range(level):
            at = at + hop(lower, j)[0] * (nodes >> (lower + 1))
        return at

    def wholes_before(j):
        return j * (wholes - 1) // (stages - 1)

    def is_split(j):
        return (j < stages - 1) & (wholes_before(j + 1) == wholes_before(j))

    def split_first(j):
        return (j - wholes_before(j)) * fs

    def whole_first(j):
        return (splits + wholes_before(j)) * fs

    def frequencies(owner, first):
        return x_ref.at[pl.ds(owner * f_dev + first, fs)]

    def send(j, number, source, slot, to):
        return pltpu.make_async_remote_copy(
            src_ref=source,
            dst_ref=recv.at[j, slot],
            send_sem=zs.at[j, number],
            recv_sem=zr.at[j, number],
            device_id=(me, to),
            device_id_type=MESH,
        )

    def whole_sends(j):
        first = whole_first(j)
        out = []
        for d in range(1, groups):
            to = (group + d) % groups
            out.append(send(j, d - 1, frequencies(to, first), group, to))
        return out

    def whole_arrivals(j):
        out = []
        for d in range(1, groups):
            source = (group + groups - d) % groups
            out.append(send(j, d - 1, recv.at[j, source], source, source))
        return out

    def split_sends(j):
        first = split_first(j)
        out = []
        for d in range(1, half):
            to = (rank + d) % half
            for other in range(2):
                owner = (side + other * (1 - 2 * side)) * half + to
                out.append(
                    send(j, 2 * (d - 1) + other, frequencies(owner, first), other * half + rank, side * half + to)
                )
        return out

    def split_arrivals(j):
        out = []
        for d in range(1, half):
            source = (rank + half - d) % half
            for other in range(2):
                place = other * half + source
                out.append(send(j, 2 * (d - 1) + other, recv.at[j, place], place, side * half + source))
        return out

    def whole_own(j):
        return [
            pltpu.make_async_copy(frequencies(group, whole_first(j)), recv.at[j, group], own_sem.at[j, 0])
        ]

    def split_own(j):
        return [
            pltpu.make_async_copy(frequencies(group, split_first(j)), recv.at[j, rank], own_sem.at[j, 0]),
            pltpu.make_async_copy(
                frequencies(counterpart, split_first(j)), recv.at[j, half + rank], own_sem.at[j, 1]
            ),
        ]

    def partial_copy(j):
        place = pl.ds(split_first(j), fs)
        return pltpu.make_async_remote_copy(
            src_ref=out_part.at[place],
            dst_ref=in_part.at[place],
            send_sem=ps.at[j],
            recv_sem=pr.at[j],
            device_id=(me, counterpart),
            device_id_type=MESH,
        )

    def by_kind(j, on_split, on_whole):
        split = is_split(j)
        pl.when(split)(functools.partial(on_split, j))
        pl.when(jnp.logical_not(split))(functools.partial(on_whole, j))

    def reduce_copy(level, j):
        bit, peer = hop(level, j)
        size = nodes >> (level + 1)
        return pltpu.make_async_remote_copy(
            src_ref=part.at[j, pl.ds(offset(level, j) + (1 - bit) * size, size)],
            dst_ref=land[level].at[j],
            send_sem=rs.at[level, j],
            recv_sem=rr.at[level, j],
            device_id=(peer, group),
            device_id_type=MESH,
        )

    def gather_copy(level, j, arrival=False):
        bit, peer = hop(level, j)
        size = nodes >> (level + 1)
        side_at = 1 - bit if arrival else bit
        place = full.at[j, pl.ds(offset(level, j) + side_at * size, size)]
        return pltpu.make_async_remote_copy(
            src_ref=place,
            dst_ref=place,
            send_sem=gs.at[level, j],
            recv_sem=gr.at[level, j],
            device_id=(peer, group),
            device_id_type=MESH,
        )

    barrier = pltpu.get_barrier_semaphore()
    for level in range(levels):
        pl.semaphore_signal(barrier, inc=1, device_id=(peer_at(2**level)[1], group), device_id_type=MESH)
    for d in range(1, groups):
        pl.semaphore_signal(barrier, inc=1, device_id=(me, (group + d) % groups), device_id_type=MESH)
    pl.semaphore_wait(barrier, levels + groups - 1)

    def start_split(j):
        for copy in split_sends(j) + split_own(j):
            copy.start()

    def start_whole(j):
        for copy in whole_sends(j) + whole_own(j):
            copy.start()

    @pl.loop(0, min(AHEAD, stages))
    def _(j):
        by_kind(j, start_split, start_whole)

    for r in range(rounds):
        at = block_ref[r] * SB - me * receivers
        column = lax.broadcasted_iota(jnp.int32, (SB, receivers), 1)
        row = lax.broadcasted_iota(jnp.int32, (SB, receivers), 0)
        sel_ref[pl.ds(r * SB, SB)] = jnp.where(column == row + at, 1.0, 0.0).astype(jnp.bfloat16)
    weights = taper_weights(window_ref[...])
    low, high = weights[:, :mid], weights[:, mid:]
    here = jnp.where(side == 0, low, high)
    weight_ref[0] = weights
    weight_ref[1] = jnp.concatenate((here, here), axis=1)

    def pick(j, kind):
        for f in range(fs):
            for c in range(2):
                block = recv[j, :, f, c].reshape(shots, receivers)
                picked = lax.dot_general(
                    sel_ref[...], block, (((1,), (1,)), ((), ())),
                    preferred_element_type=jnp.float32,
                ).reshape(rounds, SB, shots)
                tapered = (picked * weight_ref[kind][:, None, :]).astype(jnp.bfloat16)
                part[j, pl.ds((f * 2 + c) * per, per)] = tapered.reshape(per, unit, shots)

    def select_split(j):
        for copy in split_own(j):
            copy.wait()
        for copy in split_arrivals(j):
            copy.wait_recv()
        pick(j, 1)

    def select_whole(j):
        for copy in whole_own(j):
            copy.wait()
        for copy in whole_arrivals(j):
            copy.wait_recv()
        pick(j, 0)

    def select(j):
        pl.when(j + AHEAD < stages)(lambda: by_kind(j + AHEAD, start_split, start_whole))
        by_kind(j, select_split, select_whole)
        reduce_copy(0, j).start()

    def reduce(level, j):
        reduce_copy(level, j).wait_recv()
        bit, _ = hop(level, j)
        size = nodes >> (level + 1)
        kept = pl.ds(offset(level, j) + bit * size, size)
        total = part[j, kept] + land[level][j]
        if level + 1 < levels:
            part[j, kept] = total
            reduce_copy(level + 1, j).start()
        else:
            full[j, kept] = total
            gather_copy(level, j).start()

    def products(j, f, shots_at):
        first = full[j, pl.ds(2 * f * per, per)].reshape(rows, shots)[:, shots_at]
        second = full[j, pl.ds((2 * f + 1) * per, per)].reshape(rows, shots)[:, shots_at]
        both = jnp.concatenate(
            [recv[j, :, f, c].reshape(shots, receivers)[shots_at] for c in range(2)], axis=1
        )
        by_first = jnp.dot(first, both, preferred_element_type=jnp.float32)
        by_second = jnp.dot(second, both, preferred_element_type=jnp.float32)
        real = by_first[:, :receivers] + by_second[:, receivers:]
        imag = by_first[:, receivers:] - by_second[:, :receivers]
        return real, imag

    def store(at, pair):
        for c in range(2):
            out_ref[:, at, c] = (pair[c] * scale).reshape(rounds, SB, receivers).astype(jnp.bfloat16)

    def correlate_whole(j):
        for f in range(fs):
            store(whole_first(j) + f, products(j, f, slice(None)))

    def correlate_split(j):
        for f in range(fs):
            at = split_first(j) + f
            pair = products(j, f, slice(mid, None))
            for c in range(2):
                out_part[at, c] = pair[c].astype(jnp.bfloat16)
        partial_copy(j).start()
        for f in range(fs):
            at = split_first(j) + f
            pair = products(j, f, slice(0, mid))
            for c in range(2):
                acc[at, c] = pair[c]

    def correlate(j):
        by_kind(j, correlate_split, correlate_whole)

    def combine(j):
        partial_copy(j).wait_recv()
        for f in range(fs):
            at = split_first(j) + f
            store(at, [acc[at, c] + in_part[at, c].astype(jnp.float32) for c in range(2)])

    def gather(level, j):
        gather_copy(level, j, arrival=True).wait_recv()
        if level:
            gather_copy(level - 1, j).start()
        else:
            correlate(j)

    steps = [select]
    steps += [functools.partial(reduce, level) for level in range(levels)]
    steps += [functools.partial(gather, level) for level in reversed(range(levels))]

    last = SPACING * (len(steps) - 1) + LATER

    @pl.loop(0, stages + last)
    def _(tick):
        for place in [*reversed(range(1, len(steps) - 1)), len(steps) - 1, 0]:
            j = tick - SPACING * place
            pl.when((j >= 0) & (j < stages))(functools.partial(steps[place], j))
        j = tick - last
        pl.when((j >= 0) & (j < stages) & is_split(j))(functools.partial(combine, j))

    def sent_split(j):
        for copy in split_sends(j) + [partial_copy(j)]:
            copy.wait_send()

    def sent_whole(j):
        for copy in whole_sends(j):
            copy.wait_send()

    @pl.loop(0, stages)
    def _(j):
        by_kind(j, sent_split, sent_whole)
        for level in range(levels):
            reduce_copy(level, j).wait_send()
            gather_copy(level, j).wait_send()


def body(spectra, source_block, taper_window):
    f_all, parts, shot_dev, node_dev = spectra.shape
    nodes = lax.axis_size("node")
    groups = lax.axis_size("shot")
    levels = nodes.bit_length() - 1
    rounds = source_block.shape[0]
    f_dev = f_all // groups
    shots = shot_dev * groups
    rows = rounds * SB
    fs = max(1, nodes // 8)
    stages = f_dev // fs
    splits = stages // 2
    unit = fs * parts * rows // nodes
    scale = 1.0 / float(shots) ** 0.5

    bf = jnp.bfloat16
    dma = pltpu.SemaphoreType.DMA
    return pl.pallas_call(
        functools.partial(kernel, nodes, groups, stages, scale),
        out_shape=jax.ShapeDtypeStruct((rounds, f_dev, parts, SB, node_dev), bf),
        in_specs=[
            pl.BlockSpec(memory_space=pltpu.SMEM),
            pl.BlockSpec(memory_space=pltpu.VMEM),
            pl.BlockSpec(memory_space=pl.ANY),
        ],
        out_specs=pl.BlockSpec(memory_space=pltpu.VMEM),
        scratch_shapes=[
            pltpu.VMEM((rows, node_dev), bf),
            pltpu.VMEM((2, rounds, shots), jnp.float32),
            pltpu.VMEM((stages, groups, fs, parts, shot_dev, node_dev), bf),
            pltpu.VMEM((stages, nodes, unit, shots), bf),
            pltpu.VMEM((stages, nodes, unit, shots), bf),
            pltpu.VMEM((splits * fs, parts, rows, node_dev), jnp.float32),
            pltpu.VMEM((splits * fs, parts, rows, node_dev), bf),
            pltpu.VMEM((splits * fs, parts, rows, node_dev), bf),
            *[pltpu.VMEM((stages, nodes >> (level + 1), unit, shots), bf) for level in range(levels)],
            dma((stages, 2)),
            dma((stages, groups - 1)),
            dma((stages, groups - 1)),
            dma((levels, stages)),
            dma((levels, stages)),
            dma((levels, stages)),
            dma((levels, stages)),
            dma((stages,)),
            dma((stages,)),
        ],
        compiler_params=pltpu.CompilerParams(
            collective_id=0, has_side_effects=True, vmem_limit_bytes=51 * 1024 * 1024
        ),
        cost_estimate=pl.CostEstimate(
            flops=2 * 5 * f_dev * rows * shots * node_dev * 2, bytes_accessed=spectra.size * 4, transcendentals=0
        ),
    )(source_block, taper_window, spectra)


def solution(mesh):
    in_specs = (P(None, None, "shot", "node"), P(), P())
    out_specs = P(None, "shot", None, None, "node")
    return jax.shard_map(body, mesh=mesh, in_specs=in_specs, out_specs=out_specs, check_vma=False)
```

```python
import functools

import jax
import jax.numpy as jnp
from jax import lax
from jax.experimental import pallas as pl
from jax.experimental.pallas import tpu as pltpu
from jax.sharding import PartitionSpec as P

SB = 32
WINDOWS = 8
MESH = pl.DeviceIdType.MESH
AHEAD = 16
LATER = 6


def taper_weights(taper_windows):
    return 0.5 - 0.5 * jnp.cos(jnp.pi * (taper_windows.astype(jnp.float32) + 1.0) / (WINDOWS + 1.0))


def kernel(
    nodes, groups, stages, scale,
    block_ref, window_ref, x_ref, out_ref,
    sel_ref, weight_ref, recv, part, full, acc, out_part, in_part, *rest,
):
    levels = nodes.bit_length() - 1
    land = rest[:levels]
    own_sem, zs, zr, rs, rr, gs, gr, ps, pr = rest[levels:]
    me = lax.axis_index("node")
    group = lax.axis_index("shot")
    half = groups // 2
    side, rank = group // half, group % half
    counterpart = (1 - side) * half + rank
    fs = recv.shape[2]
    f_dev = stages * fs
    splits = acc.shape[0] // fs
    wholes = stages - splits
    mid = part.shape[-1] // 2
    rows = sel_ref.shape[0]
    shots = part.shape[-1]
    unit = part.shape[2]
    per = rows // unit
    rounds = rows // SB
    receivers = recv.shape[-1]

    def peer_at(stride):
        bit = (me // stride) % 2
        return bit, me + stride * (1 - 2 * bit)

    def hop(level, j):
        bit, peer = peer_at(2**level)
        if level:
            bit_odd, peer_odd = peer_at(2 ** (levels - level))
            odd = j % 2
            bit = bit + odd * (bit_odd - bit)
            peer = peer + odd * (peer_odd - peer)
        return bit, peer

    def offset(level, j):
        at = 0
        for lower in range(level):
            at = at + hop(lower, j)[0] * (nodes >> (lower + 1))
        return at

    def wholes_before(j):
        return j * (wholes - 1) // (stages - 1)

    def is_split(j):
        return (j < stages - 1) & (wholes_before(j + 1) == wholes_before(j))

    def split_first(j):
        return (j - wholes_before(j)) * fs

    def whole_first(j):
        return (splits + wholes_before(j)) * fs

    def frequencies(owner, first):
        return x_ref.at[pl.ds(owner * f_dev + first, fs)]

    def send(j, number, source, slot, to):
        return pltpu.make_async_remote_copy(
            src_ref=source,
            dst_ref=recv.at[j, slot],
            send_sem=zs.at[j, number],
            recv_sem=zr.at[j, number],
            device_id=(me, to),
            device_id_type=MESH,
        )

    def whole_sends(j):
        first = whole_first(j)
        out = []
        for d in range(1, groups):
            to = (group + d) % groups
            out.append(send(j, d - 1, frequencies(to, first), group, to))
        return out

    def whole_arrivals(j):
        out = []
        for d in range(1, groups):
            source = (group + groups - d) % groups
            out.append(send(j, d - 1, recv.at[j, source], source, source))
        return out

    def split_sends(j):
        first = split_first(j)
        out = []
        for d in range(1, half):
            to = (rank + d) % half
            for other in range(2):
                owner = (side + other * (1 - 2 * side)) * half + to
                out.append(
                    send(j, 2 * (d - 1) + other, frequencies(owner, first), other * half + rank, side * half + to)
                )
        return out

    def split_arrivals(j):
        out = []
        for d in range(1, half):
            source = (rank + half - d) % half
            for other in range(2):
                place = other * half + source
                out.append(send(j, 2 * (d - 1) + other, recv.at[j, place], place, side * half + source))
        return out

    def whole_own(j):
        return [
            pltpu.make_async_copy(frequencies(group, whole_first(j)), recv.at[j, group], own_sem.at[j, 0])
        ]

    def split_own(j):
        return [
            pltpu.make_async_copy(frequencies(group, split_first(j)), recv.at[j, rank], own_sem.at[j, 0]),
            pltpu.make_async_copy(
                frequencies(counterpart, split_first(j)), recv.at[j, half + rank], own_sem.at[j, 1]
            ),
        ]

    def partial_copy(j):
        place = pl.ds(split_first(j), fs)
        return pltpu.make_async_remote_copy(
            src_ref=out_part.at[place],
            dst_ref=in_part.at[place],
            send_sem=ps.at[j],
            recv_sem=pr.at[j],
            device_id=(me, counterpart),
            device_id_type=MESH,
        )

    def by_kind(j, on_split, on_whole):
        split = is_split(j)
        pl.when(split)(functools.partial(on_split, j))
        pl.when(jnp.logical_not(split))(functools.partial(on_whole, j))

    def reduce_copy(level, j):
        bit, peer = hop(level, j)
        size = nodes >> (level + 1)
        return pltpu.make_async_remote_copy(
            src_ref=part.at[j, pl.ds(offset(level, j) + (1 - bit) * size, size)],
            dst_ref=land[level].at[j],
            send_sem=rs.at[level, j],
            recv_sem=rr.at[level, j],
            device_id=(peer, group),
            device_id_type=MESH,
        )

    def gather_copy(level, j, arrival=False):
        bit, peer = hop(level, j)
        size = nodes >> (level + 1)
        side_at = 1 - bit if arrival else bit
        place = full.at[j, pl.ds(offset(level, j) + side_at * size, size)]
        return pltpu.make_async_remote_copy(
            src_ref=place,
            dst_ref=place,
            send_sem=gs.at[level, j],
            recv_sem=gr.at[level, j],
            device_id=(peer, group),
            device_id_type=MESH,
        )

    barrier = pltpu.get_barrier_semaphore()
    for level in range(levels):
        pl.semaphore_signal(barrier, inc=1, device_id=(peer_at(2**level)[1], group), device_id_type=MESH)
    for d in range(1, groups):
        pl.semaphore_signal(barrier, inc=1, device_id=(me, (group + d) % groups), device_id_type=MESH)
    pl.semaphore_wait(barrier, levels + groups - 1)

    def start_split(j):
        for copy in split_sends(j) + split_own(j):
            copy.start()

    def start_whole(j):
        for copy in whole_sends(j) + whole_own(j):
            copy.start()

    @pl.loop(0, min(AHEAD, stages))
    def _(j):
        by_kind(j, start_split, start_whole)

    for r in range(rounds):
        at = block_ref[r] * SB - me * receivers
        column = lax.broadcasted_iota(jnp.int32, (SB, receivers), 1)
        row = lax.broadcasted_iota(jnp.int32, (SB, receivers), 0)
        sel_ref[pl.ds(r * SB, SB)] = jnp.where(column == row + at, 1.0, 0.0).astype(jnp.bfloat16)
    weights = taper_weights(window_ref[...])
    low, high = weights[:, :mid], weights[:, mid:]
    here = jnp.where(side == 0, low, high)
    weight_ref[0] = weights
    weight_ref[1] = jnp.concatenate((here, here), axis=1)

    def pick(j, kind):
        for f in range(fs):
            for c in range(2):
                block = recv[j, :, f, c].reshape(shots, receivers)
                picked = lax.dot_general(
                    sel_ref[...], block, (((1,), (1,)), ((), ())),
                    preferred_element_type=jnp.float32,
                ).reshape(rounds, SB, shots)
                tapered = (picked * weight_ref[kind][:, None, :]).astype(jnp.bfloat16)
                part[j, pl.ds((f * 2 + c) * per, per)] = tapered.reshape(per, unit, shots)

    def select_split(j):
        for copy in split_own(j):
            copy.wait()
        for copy in split_arrivals(j):
            copy.wait_recv()
        pick(j, 1)

    def select_whole(j):
        for copy in whole_own(j):
            copy.wait()
        for copy in whole_arrivals(j):
            copy.wait_recv()
        pick(j, 0)

    def select(j):
        pl.when(j + AHEAD < stages)(lambda: by_kind(j + AHEAD, start_split, start_whole))
        by_kind(j, select_split, select_whole)
        reduce_copy(0, j).start()

    def reduce(level, j):
        reduce_copy(level, j).wait_recv()
        bit, _ = hop(level, j)
        size = nodes >> (level + 1)
        kept = pl.ds(offset(level, j) + bit * size, size)
        total = part[j, kept] + land[level][j]
        if level + 1 < levels:
            part[j, kept] = total
            reduce_copy(level + 1, j).start()
        else:
            full[j, kept] = total
            gather_copy(level, j).start()

    def products(j, f, shots_at):
        first = full[j, pl.ds(2 * f * per, per)].reshape(rows, shots)[:, shots_at]
        second = full[j, pl.ds((2 * f + 1) * per, per)].reshape(rows, shots)[:, shots_at]
        both = jnp.concatenate(
            [recv[j, :, f, c].reshape(shots, receivers)[shots_at] for c in range(2)], axis=1
        )
        by_first = jnp.dot(first, both, preferred_element_type=jnp.float32)
        by_second = jnp.dot(second, both, preferred_element_type=jnp.float32)
        real = by_first[:, :receivers] + by_second[:, receivers:]
        imag = by_first[:, receivers:] - by_second[:, :receivers]
        return real, imag

    def store(at, pair):
        for c in range(2):
            out_ref[:, at, c] = (pair[c] * scale).reshape(rounds, SB, receivers).astype(jnp.bfloat16)

    def correlate_whole(j):
        for f in range(fs):
            store(whole_first(j) + f, products(j, f, slice(None)))

    def correlate_split(j):
        for f in range(fs):
            at = split_first(j) + f
            pair = products(j, f, slice(mid, None))
            for c in range(2):
                out_part[at, c] = pair[c].astype(jnp.bfloat16)
        partial_copy(j).start()
        for f in range(fs):
            at = split_first(j) + f
            pair = products(j, f, slice(0, mid))
            for c in range(2):
                acc[at, c] = pair[c]

    def correlate(j):
        by_kind(j, correlate_split, correlate_whole)

    def combine(j):
        partial_copy(j).wait_recv()
        for f in range(fs):
            at = split_first(j) + f
            store(at, [acc[at, c] + in_part[at, c].astype(jnp.float32) for c in range(2)])

    def gather(level, j):
        gather_copy(level, j, arrival=True).wait_recv()
        if level:
            gather_copy(level - 1, j).start()
        else:
            correlate(j)

    steps = [select]
    steps += [functools.partial(reduce, level) for level in range(levels)]
    steps += [functools.partial(gather, level) for level in reversed(range(levels))]

    at_tick = [0]
    for step in range(1, len(steps)):
        at_tick.append(at_tick[-1] + (1 if step in (1, levels, levels + 1, 2 * levels) else 2))
    last = at_tick[-1] + LATER

    @pl.loop(0, stages + last)
    def _(tick):
        for place in [*reversed(range(1, len(steps) - 1)), len(steps) - 1, 0]:
            j = tick - at_tick[place]
            pl.when((j >= 0) & (j < stages))(functools.partial(steps[place], j))
        j = tick - last
        pl.when((j >= 0) & (j < stages) & is_split(j))(functools.partial(combine, j))

    def sent_split(j):
        for copy in split_sends(j) + [partial_copy(j)]:
            copy.wait_send()

    def sent_whole(j):
        for copy in whole_sends(j):
            copy.wait_send()

    @pl.loop(0, stages)
    def _(j):
        by_kind(j, sent_split, sent_whole)
        for level in range(levels):
            reduce_copy(level, j).wait_send()
            gather_copy(level, j).wait_send()


def body(spectra, source_block, taper_window):
    f_all, parts, shot_dev, node_dev = spectra.shape
    nodes = lax.axis_size("node")
    groups = lax.axis_size("shot")
    levels = nodes.bit_length() - 1
    rounds = source_block.shape[0]
    f_dev = f_all // groups
    shots = shot_dev * groups
    rows = rounds * SB
    fs = max(1, nodes // 8)
    stages = f_dev // fs
    splits = stages // 2
    unit = fs * parts * rows // nodes
    scale = 1.0 / float(shots) ** 0.5

    bf = jnp.bfloat16
    dma = pltpu.SemaphoreType.DMA
    return pl.pallas_call(
        functools.partial(kernel, nodes, groups, stages, scale),
        out_shape=jax.ShapeDtypeStruct((rounds, f_dev, parts, SB, node_dev), bf),
        in_specs=[
            pl.BlockSpec(memory_space=pltpu.SMEM),
            pl.BlockSpec(memory_space=pltpu.VMEM),
            pl.BlockSpec(memory_space=pl.ANY),
        ],
        out_specs=pl.BlockSpec(memory_space=pltpu.VMEM),
        scratch_shapes=[
            pltpu.VMEM((rows, node_dev), bf),
            pltpu.VMEM((2, rounds, shots), jnp.float32),
            pltpu.VMEM((stages, groups, fs, parts, shot_dev, node_dev), bf),
            pltpu.VMEM((stages, nodes, unit, shots), bf),
            pltpu.VMEM((stages, nodes, unit, shots), bf),
            pltpu.VMEM((splits * fs, parts, rows, node_dev), jnp.float32),
            pltpu.VMEM((splits * fs, parts, rows, node_dev), bf),
            pltpu.VMEM((splits * fs, parts, rows, node_dev), bf),
            *[pltpu.VMEM((stages, nodes >> (level + 1), unit, shots), bf) for level in range(levels)],
            dma((stages, 2)),
            dma((stages, groups - 1)),
            dma((stages, groups - 1)),
            dma((levels, stages)),
            dma((levels, stages)),
            dma((levels, stages)),
            dma((levels, stages)),
            dma((stages,)),
            dma((stages,)),
        ],
        compiler_params=pltpu.CompilerParams(
            collective_id=0, has_side_effects=True, vmem_limit_bytes=51 * 1024 * 1024
        ),
        cost_estimate=pl.CostEstimate(
            flops=2 * 5 * f_dev * rows * shots * node_dev * 2, bytes_accessed=spectra.size * 4, transcendentals=0
        ),
    )(source_block, taper_window, spectra)


def solution(mesh):
    in_specs = (P(None, None, "shot", "node"), P(), P())
    out_specs = P(None, "shot", None, None, "node")
    return jax.shard_map(body, mesh=mesh, in_specs=in_specs, out_specs=out_specs, check_vma=False)
```

```python
import functools

import jax
import jax.numpy as jnp
from jax import lax
from jax.experimental import pallas as pl
from jax.experimental.pallas import tpu as pltpu
from jax.sharding import PartitionSpec as P

SB = 32
WINDOWS = 8
MESH = pl.DeviceIdType.MESH
AHEAD = 16
SPACING = 2
LATER = 5
PIECES = 2


def taper_weights(taper_windows):
    return 0.5 - 0.5 * jnp.cos(jnp.pi * (taper_windows.astype(jnp.float32) + 1.0) / (WINDOWS + 1.0))


def kernel(
    nodes, groups, stages, scale,
    block_ref, window_ref, x_ref, out_ref,
    sel_ref, weight_ref, recv, part, full, acc, out_part, in_part, *rest,
):
    levels = nodes.bit_length() - 1
    land = rest[:levels]
    own_sem, zs, zr, rs, rr, gs, gr, ps, pr = rest[levels:]
    me = lax.axis_index("node")
    group = lax.axis_index("shot")
    half = groups // 2
    side, rank = group // half, group % half
    counterpart = (1 - side) * half + rank
    fs = recv.shape[1]
    f_dev = stages * fs
    halves = stages // 2
    mid = part.shape[-1] // 2
    rows = sel_ref.shape[0]
    shots = part.shape[-1]
    unit = part.shape[2]
    per = rows // unit
    rounds = rows // SB
    receivers = recv.shape[-1]

    def peer_at(stride):
        bit = (me // stride) % 2
        return bit, me + stride * (1 - 2 * bit)

    def hop(level, j):
        bit, peer = peer_at(2**level)
        if level:
            bit_odd, peer_odd = peer_at(2 ** (levels - level))
            odd = j % 2
            bit = bit + odd * (bit_odd - bit)
            peer = peer + odd * (peer_odd - peer)
        return bit, peer

    def offset(level, j):
        at = 0
        for lower in range(level):
            at = at + hop(lower, j)[0] * (nodes >> (lower + 1))
        return at

    def is_split(j):
        return (j == 0) | ((j % 2 == 1) & (j < stages - 1))

    def split_first(j):
        return (j + 1) // 2 * fs

    def whole_first(j):
        return (halves + (j + 1) // 2 - 1) * fs

    def frequencies(owner, first):
        return x_ref.at[pl.ds(owner * f_dev + first, fs)]

    def send(j, number, source, slot, to):
        return pltpu.make_async_remote_copy(
            src_ref=source,
            dst_ref=recv.at[j, :, :, slot],
            send_sem=zs.at[j, number],
            recv_sem=zr.at[j, number],
            device_id=(me, to),
            device_id_type=MESH,
        )

    def whole_sends(j):
        first = whole_first(j)
        out = []
        for d in range(1, groups):
            to = (group + d) % groups
            out.append(send(j, d - 1, frequencies(to, first), group, to))
        return out

    def whole_arrivals(j):
        out = []
        for d in range(1, groups):
            source = (group + groups - d) % groups
            out.append(send(j, d - 1, recv.at[j, :, :, source], source, source))
        return out

    def split_sends(j):
        first = split_first(j)
        out = []
        for d in range(1, half):
            to = (rank + d) % half
            for other in range(2):
                owner = (side + other * (1 - 2 * side)) * half + to
                out.append(
                    send(j, 2 * (d - 1) + other, frequencies(owner, first), other * half + rank, side * half + to)
                )
        return out

    def split_arrivals(j):
        out = []
        for d in range(1, half):
            source = (rank + half - d) % half
            for other in range(2):
                place = other * half + source
                out.append(send(j, 2 * (d - 1) + other, recv.at[j, :, :, place], place, side * half + source))
        return out

    def whole_own(j):
        return [
            pltpu.make_async_copy(frequencies(group, whole_first(j)), recv.at[j, :, :, group], own_sem.at[j, 0])
        ]

    def split_own(j):
        return [
            pltpu.make_async_copy(frequencies(group, split_first(j)), recv.at[j, :, :, rank], own_sem.at[j, 0]),
            pltpu.make_async_copy(
                frequencies(counterpart, split_first(j)), recv.at[j, :, :, half + rank], own_sem.at[j, 1]
            ),
        ]

    def partial_copy(j):
        place = pl.ds(split_first(j), fs)
        return pltpu.make_async_remote_copy(
            src_ref=out_part.at[place],
            dst_ref=in_part.at[place],
            send_sem=ps.at[j],
            recv_sem=pr.at[j],
            device_id=(me, counterpart),
            device_id_type=MESH,
        )

    def by_kind(j, on_split, on_whole):
        split = is_split(j)
        pl.when(split)(functools.partial(on_split, j))
        pl.when(jnp.logical_not(split))(functools.partial(on_whole, j))

    def pieces(level):
        size = nodes >> (level + 1)
        count = PIECES if level == 0 else 1
        return [(n, n * size // count, size // count) for n in range(count)]

    def reduce_copies(level, j):
        bit, peer = hop(level, j)
        start = offset(level, j) + (1 - bit) * (nodes >> (level + 1))
        return [
            pltpu.make_async_remote_copy(
                src_ref=part.at[j, pl.ds(start + at, size)],
                dst_ref=land[level].at[j, pl.ds(at, size)],
                send_sem=rs.at[level, j, n],
                recv_sem=rr.at[level, j, n],
                device_id=(peer, group),
                device_id_type=MESH,
            )
            for n, at, size in pieces(level)
        ]

    def gather_copies(level, j, arrival=False):
        bit, peer = hop(level, j)
        side_at = 1 - bit if arrival else bit
        start = offset(level, j) + side_at * (nodes >> (level + 1))
        out = []
        for n, at, size in pieces(level):
            place = full.at[j, pl.ds(start + at, size)]
            out.append(
                pltpu.make_async_remote_copy(
                    src_ref=place,
                    dst_ref=place,
                    send_sem=gs.at[level, j, n],
                    recv_sem=gr.at[level, j, n],
                    device_id=(peer, group),
                    device_id_type=MESH,
                )
            )
        return out

    def start_all(copies):
        for copy in copies:
            copy.start()

    barrier = pltpu.get_barrier_semaphore()
    for level in range(levels):
        pl.semaphore_signal(barrier, inc=1, device_id=(peer_at(2**level)[1], group), device_id_type=MESH)
    for d in range(1, groups):
        pl.semaphore_signal(barrier, inc=1, device_id=(me, (group + d) % groups), device_id_type=MESH)
    pl.semaphore_wait(barrier, levels + groups - 1)

    def start_split(j):
        for copy in split_sends(j) + split_own(j):
            copy.start()

    def start_whole(j):
        for copy in whole_sends(j) + whole_own(j):
            copy.start()

    @pl.loop(0, min(AHEAD, stages))
    def _(j):
        by_kind(j, start_split, start_whole)

    for r in range(rounds):
        at = block_ref[r] * SB - me * receivers
        column = lax.broadcasted_iota(jnp.int32, (SB, receivers), 1)
        row = lax.broadcasted_iota(jnp.int32, (SB, receivers), 0)
        sel_ref[pl.ds(r * SB, SB)] = jnp.where(column == row + at, 1.0, 0.0).astype(jnp.bfloat16)
    weights = taper_weights(window_ref[...])
    low, high = weights[:, :mid], weights[:, mid:]
    here = jnp.where(side == 0, low, high)
    weight_ref[0] = weights
    weight_ref[1] = jnp.concatenate((here, here), axis=1)

    def pick(j, kind):
        for f in range(fs):
            for c in range(2):
                block = recv[j, f, c].reshape(shots, receivers)
                picked = lax.dot_general(
                    sel_ref[...], block, (((1,), (1,)), ((), ())),
                    preferred_element_type=jnp.float32,
                ).reshape(rounds, SB, shots)
                tapered = (picked * weight_ref[kind][:, None, :]).astype(jnp.bfloat16)
                part[j, pl.ds((f * 2 + c) * per, per)] = tapered.reshape(per, unit, shots)

    def select_split(j):
        for copy in split_own(j):
            copy.wait()
        for copy in split_arrivals(j):
            copy.wait_recv()
        pick(j, 1)

    def select_whole(j):
        for copy in whole_own(j):
            copy.wait()
        for copy in whole_arrivals(j):
            copy.wait_recv()
        pick(j, 0)

    def select(j):
        pl.when(j + AHEAD < stages)(lambda: by_kind(j + AHEAD, start_split, start_whole))
        by_kind(j, select_split, select_whole)
        start_all(reduce_copies(0, j))

    def reduce(level, j):
        for copy in reduce_copies(level, j):
            copy.wait_recv()
        bit, _ = hop(level, j)
        size = nodes >> (level + 1)
        kept = pl.ds(offset(level, j) + bit * size, size)
        total = part[j, kept] + land[level][j]
        if level + 1 < levels:
            part[j, kept] = total
            start_all(reduce_copies(level + 1, j))
        else:
            full[j, kept] = total
            start_all(gather_copies(level, j))

    def products(j, f, shots_at):
        first = full[j, pl.ds(2 * f * per, per)].reshape(rows, shots)[:, shots_at]
        second = full[j, pl.ds((2 * f + 1) * per, per)].reshape(rows, shots)[:, shots_at]
        both = jnp.concatenate(
            [recv[j, f, c].reshape(shots, receivers)[shots_at] for c in range(2)], axis=1
        )
        by_first = jnp.dot(first, both, preferred_element_type=jnp.float32)
        by_second = jnp.dot(second, both, preferred_element_type=jnp.float32)
        real = by_first[:, :receivers] + by_second[:, receivers:]
        imag = by_first[:, receivers:] - by_second[:, :receivers]
        return real, imag

    def store(at, pair):
        for c in range(2):
            out_ref[:, at, c] = (pair[c] * scale).reshape(rounds, SB, receivers).astype(jnp.bfloat16)

    def correlate_whole(j):
        for f in range(fs):
            store(whole_first(j) + f, products(j, f, slice(None)))

    def correlate_split(j):
        for f in range(fs):
            at = split_first(j) + f
            pair = products(j, f, slice(mid, None))
            for c in range(2):
                out_part[at, c] = pair[c].astype(jnp.bfloat16)
        partial_copy(j).start()
        for f in range(fs):
            at = split_first(j) + f
            pair = products(j, f, slice(0, mid))
            for c in range(2):
                acc[at, c] = pair[c]

    def correlate(j):
        by_kind(j, correlate_split, correlate_whole)

    def combine(j):
        partial_copy(j).wait_recv()
        for f in range(fs):
            at = split_first(j) + f
            store(at, [acc[at, c] + in_part[at, c].astype(jnp.float32) for c in range(2)])

    def gather(level, j):
        for copy in gather_copies(level, j, arrival=True):
            copy.wait_recv()
        if level:
            start_all(gather_copies(level - 1, j))
        else:
            correlate(j)

    steps = [select]
    steps += [functools.partial(reduce, level) for level in range(levels)]
    steps += [functools.partial(gather, level) for level in reversed(range(levels))]

    last = SPACING * (len(steps) - 1) + LATER

    @pl.loop(0, stages + last)
    def _(tick):
        for place in reversed(range(len(steps))):
            j = tick - SPACING * place
            pl.when((j >= 0) & (j < stages))(functools.partial(steps[place], j))
        j = tick - last
        pl.when((j >= 0) & (j < stages) & is_split(j))(functools.partial(combine, j))

    def sent_split(j):
        for copy in split_sends(j) + [partial_copy(j)]:
            copy.wait_send()

    def sent_whole(j):
        for copy in whole_sends(j):
            copy.wait_send()

    @pl.loop(0, stages)
    def _(j):
        by_kind(j, sent_split, sent_whole)
        for level in range(levels):
            for copy in reduce_copies(level, j) + gather_copies(level, j):
                copy.wait_send()


def body(spectra, source_block, taper_window):
    f_all, parts, shot_dev, node_dev = spectra.shape
    nodes = lax.axis_size("node")
    groups = lax.axis_size("shot")
    levels = nodes.bit_length() - 1
    rounds = source_block.shape[0]
    f_dev = f_all // groups
    shots = shot_dev * groups
    rows = rounds * SB
    fs = max(1, nodes // 8)
    stages = f_dev // fs
    unit = fs * parts * rows // nodes
    scale = 1.0 / float(shots) ** 0.5

    bf = jnp.bfloat16
    dma = pltpu.SemaphoreType.DMA
    return pl.pallas_call(
        functools.partial(kernel, nodes, groups, stages, scale),
        out_shape=jax.ShapeDtypeStruct((rounds, f_dev, parts, SB, node_dev), bf),
        in_specs=[
            pl.BlockSpec(memory_space=pltpu.SMEM),
            pl.BlockSpec(memory_space=pltpu.VMEM),
            pl.BlockSpec(memory_space=pl.ANY),
        ],
        out_specs=pl.BlockSpec(memory_space=pltpu.VMEM),
        scratch_shapes=[
            pltpu.VMEM((rows, node_dev), bf),
            pltpu.VMEM((2, rounds, shots), jnp.float32),
            pltpu.VMEM((stages, fs, parts, groups, shot_dev, node_dev), bf),
            pltpu.VMEM((stages, nodes, unit, shots), bf),
            pltpu.VMEM((stages, nodes, unit, shots), bf),
            pltpu.VMEM((f_dev // 2, parts, rows, node_dev), jnp.float32),
            pltpu.VMEM((f_dev // 2, parts, rows, node_dev), bf),
            pltpu.VMEM((f_dev // 2, parts, rows, node_dev), bf),
            *[pltpu.VMEM((stages, nodes >> (level + 1), unit, shots), bf) for level in range(levels)],
            dma((stages, 2)),
            dma((stages, groups - 1)),
            dma((stages, groups - 1)),
            dma((levels, stages, PIECES)),
            dma((levels, stages, PIECES)),
            dma((levels, stages, PIECES)),
            dma((levels, stages, PIECES)),
            dma((stages,)),
            dma((stages,)),
        ],
        compiler_params=pltpu.CompilerParams(
            collective_id=0, has_side_effects=True, vmem_limit_bytes=51 * 1024 * 1024
        ),
        cost_estimate=pl.CostEstimate(
            flops=2 * 5 * f_dev * rows * shots * node_dev * 2, bytes_accessed=spectra.size * 4, transcendentals=0
        ),
    )(source_block, taper_window, spectra)


def solution(mesh):
    in_specs = (P(None, None, "shot", "node"), P(), P())
    out_specs = P(None, "shot", None, None, "node")
    return jax.shard_map(body, mesh=mesh, in_specs=in_specs, out_specs=out_specs, check_vma=False)
```

```python
import functools

import jax
import jax.numpy as jnp
from jax import lax
from jax.experimental import pallas as pl
from jax.experimental.pallas import tpu as pltpu
from jax.sharding import PartitionSpec as P

SB = 32
WINDOWS = 8
MESH = pl.DeviceIdType.MESH
AHEAD = 3
SPACING = 2
LATER = 5


def taper_weights(taper_windows):
    return 0.5 - 0.5 * jnp.cos(jnp.pi * (taper_windows.astype(jnp.float32) + 1.0) / (WINDOWS + 1.0))


def kernel(
    nodes, groups, stages, scale,
    block_ref, window_ref, x_ref, out_ref,
    sel_ref, weight_ref, recv, part, full, acc, out_part, in_part, *rest,
):
    levels = nodes.bit_length() - 1
    land = rest[:levels]
    own_sem, zs, zr, rs, rr, gs, gr, ps, pr = rest[levels:]
    me = lax.axis_index("node")
    group = lax.axis_index("shot")
    half = groups // 2
    side, rank = group // half, group % half
    counterpart = (1 - side) * half + rank
    fs = recv.shape[1]
    f_dev = stages * fs
    halves = stages // 2
    mid = part.shape[-1] // 2
    rows = sel_ref.shape[0]
    shots = part.shape[-1]
    unit = part.shape[2]
    per = rows // unit
    rounds = rows // SB
    receivers = recv.shape[-1]

    def peer_at(stride):
        bit = (me // stride) % 2
        return bit, me + stride * (1 - 2 * bit)

    def hop(level, j):
        bit, peer = peer_at(2**level)
        if level:
            bit_odd, peer_odd = peer_at(2 ** (levels - level))
            odd = j % 2
            bit = bit + odd * (bit_odd - bit)
            peer = peer + odd * (peer_odd - peer)
        return bit, peer

    def offset(level, j):
        at = 0
        for lower in range(level):
            at = at + hop(lower, j)[0] * (nodes >> (lower + 1))
        return at

    def is_split(j):
        return (j == 0) | ((j % 2 == 1) & (j < stages - 1))

    def split_first(j):
        return (j + 1) // 2 * fs

    def whole_first(j):
        return (halves + (j + 1) // 2 - 1) * fs

    def frequencies(owner, first):
        return x_ref.at[pl.ds(owner * f_dev + first, fs)]

    def send(j, number, source, slot, to):
        return pltpu.make_async_remote_copy(
            src_ref=source,
            dst_ref=recv.at[j, :, :, slot],
            send_sem=zs.at[j, number],
            recv_sem=zr.at[j, number],
            device_id=(me, to),
            device_id_type=MESH,
        )

    def whole_sends(j):
        first = whole_first(j)
        out = []
        for d in range(1, groups):
            to = (group + d) % groups
            out.append(send(j, d - 1, frequencies(to, first), group, to))
        return out

    def whole_arrivals(j):
        out = []
        for d in range(1, groups):
            source = (group + groups - d) % groups
            out.append(send(j, d - 1, recv.at[j, :, :, source], source, source))
        return out

    def split_sends(j):
        first = split_first(j)
        out = []
        for d in range(1, half):
            to = (rank + d) % half
            for other in range(2):
                owner = (side + other * (1 - 2 * side)) * half + to
                out.append(
                    send(j, 2 * (d - 1) + other, frequencies(owner, first), other * half + rank, side * half + to)
                )
        return out

    def split_arrivals(j):
        out = []
        for d in range(1, half):
            source = (rank + half - d) % half
            for other in range(2):
                place = other * half + source
                out.append(send(j, 2 * (d - 1) + other, recv.at[j, :, :, place], place, side * half + source))
        return out

    def whole_own(j):
        return [
            pltpu.make_async_copy(frequencies(group, whole_first(j)), recv.at[j, :, :, group], own_sem.at[j, 0])
        ]

    def split_own(j):
        return [
            pltpu.make_async_copy(frequencies(group, split_first(j)), recv.at[j, :, :, rank], own_sem.at[j, 0]),
            pltpu.make_async_copy(
                frequencies(counterpart, split_first(j)), recv.at[j, :, :, half + rank], own_sem.at[j, 1]
            ),
        ]

    def partial_copy(j):
        place = pl.ds(split_first(j), fs)
        return pltpu.make_async_remote_copy(
            src_ref=out_part.at[place],
            dst_ref=in_part.at[place],
            send_sem=ps.at[j],
            recv_sem=pr.at[j],
            device_id=(me, counterpart),
            device_id_type=MESH,
        )

    def by_kind(j, on_split, on_whole):
        split = is_split(j)
        pl.when(split)(functools.partial(on_split, j))
        pl.when(jnp.logical_not(split))(functools.partial(on_whole, j))

    def reduce_copy(level, j):
        bit, peer = hop(level, j)
        size = nodes >> (level + 1)
        return pltpu.make_async_remote_copy(
            src_ref=part.at[j, pl.ds(offset(level, j) + (1 - bit) * size, size)],
            dst_ref=land[level].at[j],
            send_sem=rs.at[level, j],
            recv_sem=rr.at[level, j],
            device_id=(peer, group),
            device_id_type=MESH,
        )

    def gather_copy(level, j, arrival=False):
        bit, peer = hop(level, j)
        size = nodes >> (level + 1)
        side_at = 1 - bit if arrival else bit
        place = full.at[j, pl.ds(offset(level, j) + side_at * size, size)]
        return pltpu.make_async_remote_copy(
            src_ref=place,
            dst_ref=place,
            send_sem=gs.at[level, j],
            recv_sem=gr.at[level, j],
            device_id=(peer, group),
            device_id_type=MESH,
        )

    barrier = pltpu.get_barrier_semaphore()
    for level in range(levels):
        pl.semaphore_signal(barrier, inc=1, device_id=(peer_at(2**level)[1], group), device_id_type=MESH)
    for d in range(1, groups):
        pl.semaphore_signal(barrier, inc=1, device_id=(me, (group + d) % groups), device_id_type=MESH)
    pl.semaphore_wait(barrier, levels + groups - 1)

    def start_split(j):
        for copy in split_sends(j) + split_own(j):
            copy.start()

    def start_whole(j):
        for copy in whole_sends(j) + whole_own(j):
            copy.start()

    @pl.loop(0, min(AHEAD, stages))
    def _(j):
        by_kind(j, start_split, start_whole)

    for r in range(rounds):
        at = block_ref[r] * SB - me * receivers
        column = lax.broadcasted_iota(jnp.int32, (SB, receivers), 1)
        row = lax.broadcasted_iota(jnp.int32, (SB, receivers), 0)
        sel_ref[pl.ds(r * SB, SB)] = jnp.where(column == row + at, 1.0, 0.0).astype(jnp.bfloat16)
    weights = taper_weights(window_ref[...])
    low, high = weights[:, :mid], weights[:, mid:]
    here = jnp.where(side == 0, low, high)
    weight_ref[0] = weights
    weight_ref[1] = jnp.concatenate((here, here), axis=1)

    def pick(j, kind):
        for f in range(fs):
            for c in range(2):
                block = recv[j, f, c].reshape(shots, receivers)
                picked = lax.dot_general(
                    sel_ref[...], block, (((1,), (1,)), ((), ())),
                    preferred_element_type=jnp.float32,
                ).reshape(rounds, SB, shots)
                tapered = (picked * weight_ref[kind][:, None, :]).astype(jnp.bfloat16)
                part[j, pl.ds((f * 2 + c) * per, per)] = tapered.reshape(per, unit, shots)

    def select_split(j):
        for copy in split_own(j):
            copy.wait()
        for copy in split_arrivals(j):
            copy.wait_recv()
        pick(j, 1)

    def select_whole(j):
        for copy in whole_own(j):
            copy.wait()
        for copy in whole_arrivals(j):
            copy.wait_recv()
        pick(j, 0)

    def select(j):
        pl.when(j + AHEAD < stages)(lambda: by_kind(j + AHEAD, start_split, start_whole))
        by_kind(j, select_split, select_whole)
        reduce_copy(0, j).start()

    def reduce(level, j):
        reduce_copy(level, j).wait_recv()
        bit, _ = hop(level, j)
        size = nodes >> (level + 1)
        kept = pl.ds(offset(level, j) + bit * size, size)
        total = part[j, kept] + land[level][j]
        if level + 1 < levels:
            part[j, kept] = total
            reduce_copy(level + 1, j).start()
        else:
            full[j, kept] = total
            gather_copy(level, j).start()

    def products(j, f, shots_at):
        first = full[j, pl.ds(2 * f * per, per)].reshape(rows, shots)[:, shots_at]
        second = full[j, pl.ds((2 * f + 1) * per, per)].reshape(rows, shots)[:, shots_at]
        both = jnp.concatenate(
            [recv[j, f, c].reshape(shots, receivers)[shots_at] for c in range(2)], axis=1
        )
        by_first = jnp.dot(first, both, preferred_element_type=jnp.float32)
        by_second = jnp.dot(second, both, preferred_element_type=jnp.float32)
        real = by_first[:, :receivers] + by_second[:, receivers:]
        imag = by_first[:, receivers:] - by_second[:, :receivers]
        return real, imag

    def store(at, pair):
        for c in range(2):
            out_ref[:, at, c] = (pair[c] * scale).reshape(rounds, SB, receivers).astype(jnp.bfloat16)

    def correlate_whole(j):
        for f in range(fs):
            store(whole_first(j) + f, products(j, f, slice(None)))

    def correlate_split(j):
        for f in range(fs):
            at = split_first(j) + f
            pair = products(j, f, slice(mid, None))
            for c in range(2):
                out_part[at, c] = pair[c].astype(jnp.bfloat16)
        partial_copy(j).start()
        for f in range(fs):
            at = split_first(j) + f
            pair = products(j, f, slice(0, mid))
            for c in range(2):
                acc[at, c] = pair[c]

    def correlate(j):
        by_kind(j, correlate_split, correlate_whole)

    def combine(j):
        partial_copy(j).wait_recv()
        for f in range(fs):
            at = split_first(j) + f
            store(at, [acc[at, c] + in_part[at, c].astype(jnp.float32) for c in range(2)])

    def gather(level, j):
        gather_copy(level, j, arrival=True).wait_recv()
        if level:
            gather_copy(level - 1, j).start()
        else:
            correlate(j)

    steps = [select]
    steps += [functools.partial(reduce, level) for level in range(levels)]
    steps += [functools.partial(gather, level) for level in reversed(range(levels))]

    last = SPACING * (len(steps) - 1) + LATER

    @pl.loop(0, stages + last)
    def _(tick):
        for place in reversed(range(len(steps))):
            j = tick - SPACING * place
            pl.when((j >= 0) & (j < stages))(functools.partial(steps[place], j))
        j = tick - last
        pl.when((j >= 0) & (j < stages) & is_split(j))(functools.partial(combine, j))

    def sent_split(j):
        for copy in split_sends(j) + [partial_copy(j)]:
            copy.wait_send()

    def sent_whole(j):
        for copy in whole_sends(j):
            copy.wait_send()

    @pl.loop(0, stages)
    def _(j):
        by_kind(j, sent_split, sent_whole)
        for level in range(levels):
            reduce_copy(level, j).wait_send()
            gather_copy(level, j).wait_send()


def body(spectra, source_block, taper_window):
    f_all, parts, shot_dev, node_dev = spectra.shape
    nodes = lax.axis_size("node")
    groups = lax.axis_size("shot")
    levels = nodes.bit_length() - 1
    rounds = source_block.shape[0]
    f_dev = f_all // groups
    shots = shot_dev * groups
    rows = rounds * SB
    fs = max(1, nodes // 8)
    stages = f_dev // fs
    unit = fs * parts * rows // nodes
    scale = 1.0 / float(shots) ** 0.5

    bf = jnp.bfloat16
    dma = pltpu.SemaphoreType.DMA
    return pl.pallas_call(
        functools.partial(kernel, nodes, groups, stages, scale),
        out_shape=jax.ShapeDtypeStruct((rounds, f_dev, parts, SB, node_dev), bf),
        in_specs=[
            pl.BlockSpec(memory_space=pltpu.SMEM),
            pl.BlockSpec(memory_space=pltpu.VMEM),
            pl.BlockSpec(memory_space=pl.ANY),
        ],
        out_specs=pl.BlockSpec(memory_space=pltpu.VMEM),
        scratch_shapes=[
            pltpu.VMEM((rows, node_dev), bf),
            pltpu.VMEM((2, rounds, shots), jnp.float32),
            pltpu.VMEM((stages, fs, parts, groups, shot_dev, node_dev), bf),
            pltpu.VMEM((stages, nodes, unit, shots), bf),
            pltpu.VMEM((stages, nodes, unit, shots), bf),
            pltpu.VMEM((f_dev // 2, parts, rows, node_dev), jnp.float32),
            pltpu.VMEM((f_dev // 2, parts, rows, node_dev), bf),
            pltpu.VMEM((f_dev // 2, parts, rows, node_dev), bf),
            *[pltpu.VMEM((stages, nodes >> (level + 1), unit, shots), bf) for level in range(levels)],
            dma((stages, 2)),
            dma((stages, groups - 1)),
            dma((stages, groups - 1)),
            dma((levels, stages)),
            dma((levels, stages)),
            dma((levels, stages)),
            dma((levels, stages)),
            dma((stages,)),
            dma((stages,)),
        ],
        compiler_params=pltpu.CompilerParams(
            collective_id=0, has_side_effects=True, vmem_limit_bytes=51 * 1024 * 1024
        ),
        cost_estimate=pl.CostEstimate(
            flops=2 * 5 * f_dev * rows * shots * node_dev * 2, bytes_accessed=spectra.size * 4, transcendentals=0
        ),
    )(source_block, taper_window, spectra)


def solution(mesh):
    in_specs = (P(None, None, "shot", "node"), P(), P())
    out_specs = P(None, "shot", None, None, "node")
    return jax.shard_map(body, mesh=mesh, in_specs=in_specs, out_specs=out_specs, check_vma=False)
```

```python
import functools

import jax
import jax.numpy as jnp
from jax import lax
from jax.experimental import pallas as pl
from jax.experimental.pallas import tpu as pltpu
from jax.sharding import PartitionSpec as P

SB = 32
WINDOWS = 8
MESH = pl.DeviceIdType.MESH
AHEAD = 3
SPACING = 2
LATER = 9


def taper_weights(taper_windows):
    return 0.5 - 0.5 * jnp.cos(jnp.pi * (taper_windows.astype(jnp.float32) + 1.0) / (WINDOWS + 1.0))


def kernel(
    nodes, groups, stages, scale,
    block_ref, window_ref, x_ref, out_ref,
    sel_ref, weight_ref, recv, part, full, acc, out_part, in_part, *rest,
):
    levels = nodes.bit_length() - 1
    land = rest[:levels]
    own_sem, zs, zr, rs, rr, gs, gr, ps, pr = rest[levels:]
    me = lax.axis_index("node")
    group = lax.axis_index("shot")
    half = groups // 2
    side, rank = group // half, group % half
    counterpart = (1 - side) * half + rank
    fs = recv.shape[1]
    f_dev = stages * fs
    halves = stages // 2
    mid = part.shape[-1] // 2
    rows = sel_ref.shape[0]
    shots = part.shape[-1]
    unit = part.shape[2]
    per = rows // unit
    rounds = rows // SB
    receivers = recv.shape[-1]

    def peer_at(stride):
        bit = (me // stride) % 2
        return bit, me + stride * (1 - 2 * bit)

    def hop(level, j):
        bit, peer = peer_at(2**level)
        if level:
            bit_odd, peer_odd = peer_at(2 ** (levels - level))
            odd = j % 2
            bit = bit + odd * (bit_odd - bit)
            peer = peer + odd * (peer_odd - peer)
        return bit, peer

    def offset(level, j):
        at = 0
        for lower in range(level):
            at = at + hop(lower, j)[0] * (nodes >> (lower + 1))
        return at

    def is_split(j):
        return (j == 0) | ((j % 2 == 1) & (j < stages - 1))

    def split_first(j):
        return (j + 1) // 2 * fs

    def whole_first(j):
        return (halves + (j + 1) // 2 - 1) * fs

    def frequencies(owner, first):
        return x_ref.at[pl.ds(owner * f_dev + first, fs)]

    def send(j, number, source, slot, to):
        return pltpu.make_async_remote_copy(
            src_ref=source,
            dst_ref=recv.at[j, :, :, slot],
            send_sem=zs.at[j, number],
            recv_sem=zr.at[j, number],
            device_id=(me, to),
            device_id_type=MESH,
        )

    def whole_sends(j):
        first = whole_first(j)
        out = []
        for d in range(1, groups):
            to = (group + d) % groups
            out.append(send(j, d - 1, frequencies(to, first), group, to))
        return out

    def whole_arrivals(j):
        out = []
        for d in range(1, groups):
            source = (group + groups - d) % groups
            out.append(send(j, d - 1, recv.at[j, :, :, source], source, source))
        return out

    def split_sends(j):
        first = split_first(j)
        out = []
        for d in range(1, half):
            to = (rank + d) % half
            for other in range(2):
                owner = (side + other * (1 - 2 * side)) * half + to
                out.append(
                    send(j, 2 * (d - 1) + other, frequencies(owner, first), other * half + rank, side * half + to)
                )
        return out

    def split_arrivals(j):
        out = []
        for d in range(1, half):
            source = (rank + half - d) % half
            for other in range(2):
                place = other * half + source
                out.append(send(j, 2 * (d - 1) + other, recv.at[j, :, :, place], place, side * half + source))
        return out

    def whole_own(j):
        return [
            pltpu.make_async_copy(frequencies(group, whole_first(j)), recv.at[j, :, :, group], own_sem.at[j, 0])
        ]

    def split_own(j):
        return [
            pltpu.make_async_copy(frequencies(group, split_first(j)), recv.at[j, :, :, rank], own_sem.at[j, 0]),
            pltpu.make_async_copy(
                frequencies(counterpart, split_first(j)), recv.at[j, :, :, half + rank], own_sem.at[j, 1]
            ),
        ]

    def partial_copy(j):
        place = pl.ds(split_first(j), fs)
        return pltpu.make_async_remote_copy(
            src_ref=out_part.at[place],
            dst_ref=in_part.at[place],
            send_sem=ps.at[j],
            recv_sem=pr.at[j],
            device_id=(me, counterpart),
            device_id_type=MESH,
        )

    def by_kind(j, on_split, on_whole):
        split = is_split(j)
        pl.when(split)(functools.partial(on_split, j))
        pl.when(jnp.logical_not(split))(functools.partial(on_whole, j))

    def reduce_copy(level, j):
        bit, peer = hop(level, j)
        size = nodes >> (level + 1)
        return pltpu.make_async_remote_copy(
            src_ref=part.at[j, pl.ds(offset(level, j) + (1 - bit) * size, size)],
            dst_ref=land[level].at[j],
            send_sem=rs.at[level, j],
            recv_sem=rr.at[level, j],
            device_id=(peer, group),
            device_id_type=MESH,
        )

    def gather_copy(level, j, arrival=False):
        bit, peer = hop(level, j)
        size = nodes >> (level + 1)
        side_at = 1 - bit if arrival else bit
        place = full.at[j, pl.ds(offset(level, j) + side_at * size, size)]
        return pltpu.make_async_remote_copy(
            src_ref=place,
            dst_ref=place,
            send_sem=gs.at[level, j],
            recv_sem=gr.at[level, j],
            device_id=(peer, group),
            device_id_type=MESH,
        )

    barrier = pltpu.get_barrier_semaphore()
    for level in range(levels):
        pl.semaphore_signal(barrier, inc=1, device_id=(peer_at(2**level)[1], group), device_id_type=MESH)
    for d in range(1, groups):
        pl.semaphore_signal(barrier, inc=1, device_id=(me, (group + d) % groups), device_id_type=MESH)
    pl.semaphore_wait(barrier, levels + groups - 1)

    def start_split(j):
        for copy in split_sends(j) + split_own(j):
            copy.start()

    def start_whole(j):
        for copy in whole_sends(j) + whole_own(j):
            copy.start()

    @pl.loop(0, min(AHEAD, stages))
    def _(j):
        by_kind(j, start_split, start_whole)

    for r in range(rounds):
        at = block_ref[r] * SB - me * receivers
        column = lax.broadcasted_iota(jnp.int32, (SB, receivers), 1)
        row = lax.broadcasted_iota(jnp.int32, (SB, receivers), 0)
        sel_ref[pl.ds(r * SB, SB)] = jnp.where(column == row + at, 1.0, 0.0).astype(jnp.bfloat16)
    weights = taper_weights(window_ref[...])
    low, high = weights[:, :mid], weights[:, mid:]
    here = jnp.where(side == 0, low, high)
    weight_ref[0] = weights
    weight_ref[1] = jnp.concatenate((here, here), axis=1)

    def pick(j, kind):
        for f in range(fs):
            for c in range(2):
                block = recv[j, f, c].reshape(shots, receivers)
                picked = lax.dot_general(
                    sel_ref[...], block, (((1,), (1,)), ((), ())),
                    preferred_element_type=jnp.float32,
                ).reshape(rounds, SB, shots)
                tapered = (picked * weight_ref[kind][:, None, :]).astype(jnp.bfloat16)
                part[j, pl.ds((f * 2 + c) * per, per)] = tapered.reshape(per, unit, shots)

    def select_split(j):
        for copy in split_own(j):
            copy.wait()
        for copy in split_arrivals(j):
            copy.wait_recv()
        pick(j, 1)

    def select_whole(j):
        for copy in whole_own(j):
            copy.wait()
        for copy in whole_arrivals(j):
            copy.wait_recv()
        pick(j, 0)

    def select(j):
        pl.when(j + AHEAD < stages)(lambda: by_kind(j + AHEAD, start_split, start_whole))
        by_kind(j, select_split, select_whole)
        reduce_copy(0, j).start()

    def reduce(level, j):
        reduce_copy(level, j).wait_recv()
        bit, _ = hop(level, j)
        size = nodes >> (level + 1)
        kept = pl.ds(offset(level, j) + bit * size, size)
        total = part[j, kept] + land[level][j]
        if level + 1 < levels:
            part[j, kept] = total
            reduce_copy(level + 1, j).start()
        else:
            full[j, kept] = total
            gather_copy(level, j).start()

    def products(j, f, shots_at):
        first = full[j, pl.ds(2 * f * per, per)].reshape(rows, shots)[:, shots_at]
        second = full[j, pl.ds((2 * f + 1) * per, per)].reshape(rows, shots)[:, shots_at]
        both = jnp.concatenate(
            [recv[j, f, c].reshape(shots, receivers)[shots_at] for c in range(2)], axis=1
        )
        by_first = jnp.dot(first, both, preferred_element_type=jnp.float32)
        by_second = jnp.dot(second, both, preferred_element_type=jnp.float32)
        real = by_first[:, :receivers] + by_second[:, receivers:]
        imag = by_first[:, receivers:] - by_second[:, :receivers]
        return real, imag

    def store(at, pair):
        for c in range(2):
            out_ref[:, at, c] = (pair[c] * scale).reshape(rounds, SB, receivers).astype(jnp.bfloat16)

    def correlate_whole(j):
        for f in range(fs):
            store(whole_first(j) + f, products(j, f, slice(None)))

    def correlate_split(j):
        for f in range(fs):
            at = split_first(j) + f
            pair = products(j, f, slice(mid, None))
            for c in range(2):
                out_part[at, c] = pair[c].astype(jnp.bfloat16)
        partial_copy(j).start()
        for f in range(fs):
            at = split_first(j) + f
            pair = products(j, f, slice(0, mid))
            for c in range(2):
                acc[at, c] = pair[c]

    def correlate(j):
        by_kind(j, correlate_split, correlate_whole)

    def combine(j):
        partial_copy(j).wait_recv()
        for f in range(fs):
            at = split_first(j) + f
            store(at, [acc[at, c] + in_part[at, c].astype(jnp.float32) for c in range(2)])

    def gather(level, j):
        gather_copy(level, j, arrival=True).wait_recv()
        if level:
            gather_copy(level - 1, j).start()
        else:
            correlate(j)

    steps = [select]
    steps += [functools.partial(reduce, level) for level in range(levels)]
    steps += [functools.partial(gather, level) for level in reversed(range(levels))]

    last = SPACING * (len(steps) - 1) + LATER

    @pl.loop(0, stages + last)
    def _(tick):
        for place in reversed(range(len(steps))):
            j = tick - SPACING * place
            pl.when((j >= 0) & (j < stages))(functools.partial(steps[place], j))
        j = tick - last
        pl.when((j >= 0) & (j < stages) & is_split(j))(functools.partial(combine, j))

    def sent_split(j):
        for copy in split_sends(j) + [partial_copy(j)]:
            copy.wait_send()

    def sent_whole(j):
        for copy in whole_sends(j):
            copy.wait_send()

    @pl.loop(0, stages)
    def _(j):
        by_kind(j, sent_split, sent_whole)
        for level in range(levels):
            reduce_copy(level, j).wait_send()
            gather_copy(level, j).wait_send()


def body(spectra, source_block, taper_window):
    f_all, parts, shot_dev, node_dev = spectra.shape
    nodes = lax.axis_size("node")
    groups = lax.axis_size("shot")
    levels = nodes.bit_length() - 1
    rounds = source_block.shape[0]
    f_dev = f_all // groups
    shots = shot_dev * groups
    rows = rounds * SB
    fs = max(1, nodes // 8)
    stages = f_dev // fs
    unit = fs * parts * rows // nodes
    scale = 1.0 / float(shots) ** 0.5

    bf = jnp.bfloat16
    dma = pltpu.SemaphoreType.DMA
    return pl.pallas_call(
        functools.partial(kernel, nodes, groups, stages, scale),
        out_shape=jax.ShapeDtypeStruct((rounds, f_dev, parts, SB, node_dev), bf),
        in_specs=[
            pl.BlockSpec(memory_space=pltpu.SMEM),
            pl.BlockSpec(memory_space=pltpu.VMEM),
            pl.BlockSpec(memory_space=pl.ANY),
        ],
        out_specs=pl.BlockSpec(memory_space=pltpu.VMEM),
        scratch_shapes=[
            pltpu.VMEM((rows, node_dev), bf),
            pltpu.VMEM((2, rounds, shots), jnp.float32),
            pltpu.VMEM((stages, fs, parts, groups, shot_dev, node_dev), bf),
            pltpu.VMEM((stages, nodes, unit, shots), bf),
            pltpu.VMEM((stages, nodes, unit, shots), bf),
            pltpu.VMEM((f_dev // 2, parts, rows, node_dev), jnp.float32),
            pltpu.VMEM((f_dev // 2, parts, rows, node_dev), bf),
            pltpu.VMEM((f_dev // 2, parts, rows, node_dev), bf),
            *[pltpu.VMEM((stages, nodes >> (level + 1), unit, shots), bf) for level in range(levels)],
            dma((stages, 2)),
            dma((stages, groups - 1)),
            dma((stages, groups - 1)),
            dma((levels, stages)),
            dma((levels, stages)),
            dma((levels, stages)),
            dma((levels, stages)),
            dma((stages,)),
            dma((stages,)),
        ],
        compiler_params=pltpu.CompilerParams(
            collective_id=0, has_side_effects=True, vmem_limit_bytes=51 * 1024 * 1024
        ),
        cost_estimate=pl.CostEstimate(
            flops=2 * 5 * f_dev * rows * shots * node_dev * 2, bytes_accessed=spectra.size * 4, transcendentals=0
        ),
    )(source_block, taper_window, spectra)


def solution(mesh):
    in_specs = (P(None, None, "shot", "node"), P(), P())
    out_specs = P(None, "shot", None, None, "node")
    return jax.shard_map(body, mesh=mesh, in_specs=in_specs, out_specs=out_specs, check_vma=False)
```
